32 devices in a mesh: tile: 4 (over x, core), kern: 8 (over z, y).
Axes of the slice: x: 2, y: 2, z: 4, core: 2. Of those that a mesh axis runs over, the one named last changes fastest.
Arguments:
- mask: float32 [256, 2048], P('tile'), may hold values from 0 to 1
- target: int32 [256, 2048], P('tile'), may hold values 0 or 1
- kernels: bfloat16 [8, 2, 21, 21], P('kern'), may hold values from -0.25 to 0.25
- source_weight: float32 [8], replicated, may hold values from 0.2 to 2
- assign: int32 [8], P('kern'), may hold values from 0 to 7, each once
Outputs:
- mask_grad: float32 [256, 2048], P('tile', 'kern')
- resist: float32 [256, 2048], P('tile', 'kern')
The draws below stay inside these ranges and needn't reach their ends.
Inputs may be any that keep to these rules, and one draw needn't show every extreme that they name: assign is a permutation of 0 to 7.
All inputs are finite; a program needn't handle non-finite values. No bound on the sum of `target` on one device may be relied on, other than what follows from the above.
Results may differ from the reference program's by a relative error of at most 0.0036.
Values may be sent and summed in bfloat16 or wider, within the bound.
A program may use at most 64 MiB of HBM per device.

```python
import math
import jax
import jax.numpy as jnp
from jax import lax

KS = 21
COLS = 2048
SOURCES = 8
ROWS = 256


def with_ends(drawn, rng, low, largest):
    index_at = [jax.random.randint(jax.random.fold_in(rng, axis), (), 0, length) for axis, length in enumerate(drawn.shape)]
    main_axis = drawn.shape.index(max(drawn.shape))
    next_to = index_at[:main_axis] + [(index_at[main_axis] + 1) % drawn.shape[main_axis]] + index_at[main_axis + 1:]
    return drawn.at[tuple(index_at)].set(low).at[tuple(next_to)].set(largest)


def shard_levels(key, extent, pieces, low, largest):
    factor_of, own = 1.0, jax.random.fold_in(key, 6)
    for dim, parts in pieces:
        steps = jnp.exp(jax.random.uniform(jax.random.fold_in(own, dim), (parts,), jnp.float32, low / len(pieces), largest / len(pieces)))
        factor_of = factor_of * jnp.repeat(steps, extent[dim] // parts).reshape([-1 if axis == dim else 1 for axis in range(len(extent))])
    return factor_of


def scatter_about(stream_key, dims, spread, bound, pieces=(), held_as=jnp.bfloat16):
    level = shard_levels(stream_key, dims, pieces, -0.22, 0.18) if pieces else 1.0
    entries = jax.random.normal(stream_key, dims, jnp.float32) * spread * level
    return jnp.minimum(jnp.maximum(entries, -bound), bound).astype(held_as)


def setup_inputs(seed: int = 0) -> dict:
    streams_of = jax.random.split(jax.random.key(seed), 6)
    return {
        "mask": jnp.clip(1.0 * jax.random.uniform(streams_of[0], (ROWS, COLS), jnp.float32) ** shard_levels(streams_of[0], (ROWS, COLS), ((0, 4),), -0.2, 0.2), 0.0, 1.0),
        "target": with_ends((jax.random.randint(streams_of[1], (ROWS, COLS), 0, 2) < 1).astype(jnp.int32), jax.random.fold_in(streams_of[1], 1), 0, 1),
        "kernels": scatter_about(streams_of[2], (SOURCES, 2, KS, KS), (KS * KS) ** -0.5, 0.25, ((0, 8),)),
        "source_weight": jnp.clip(jnp.exp(jax.random.uniform(streams_of[3], (SOURCES,), jnp.float32, math.log(0.2), math.log(2.0))), 0.2, 2.0),
        "assign": jax.random.permutation(streams_of[4], SOURCES).astype(jnp.int32),
    }


def reference(mask, target, kernels, source_weight, assign):
    margin = (KS - 1) // 2
    copy_wide = mask.astype(jnp.bfloat16).astype(jnp.float32)
    weights = jnp.take(source_weight, assign.astype(jnp.int32))
    total = jnp.sum(source_weight)

    def fields_of(kernel_pair):
        rhs = kernel_pair.astype(jnp.float32)[:, None]
        out = lax.conv_general_dilated(copy_wide[None, None], rhs, (1, 1), ((margin, margin), (margin, margin)), precision=lax.Precision.HIGHEST)
        return out[0]

    def add_image(carry, packed):
        kernel_pair, weight_one = packed
        fields = fields_of(kernel_pair)
        return (carry + weight_one * (fields[0] * fields[0] + fields[1] * fields[1]), None)
    aerial, unused = lax.scan(add_image, jnp.zeros(mask.shape, jnp.float32), (kernels, weights))
    aerial = aerial / total
    resist = jax.nn.sigmoid(4.0 * (aerial - 0.6))
    sense = 2.0 * (resist - target.astype(jnp.float32)) * 4.0 * resist * (1.0 - resist)

    def add_grad(carry, packed):
        kernel_pair, weight_one = packed
        fields = fields_of(kernel_pair)
        adjoint = (2.0 * weight_one / total * sense[None] * fields).astype(jnp.bfloat16).astype(jnp.float32)
        flipped = kernel_pair[:, ::-1, ::-1].astype(jnp.float32)[None]
        out = lax.conv_general_dilated(adjoint[None], flipped, (1, 1), ((margin, margin), (margin, margin)), precision=lax.Precision.HIGHEST)
        return (carry + out[0, 0], None)
    mask_grad, unused_two = lax.scan(add_grad, jnp.zeros(mask.shape, jnp.float32), (kernels, weights))
    return (mask_grad, resist)
```

```python
import functools

import jax
import jax.numpy as jnp
from jax import lax
from jax.experimental import pallas as pl
from jax.experimental.pallas import tpu as pltpu
from jax.sharding import PartitionSpec as P

SLOPE_FACTOR = 4.0
LEVEL_VALUE = 0.6
PITCH = 64
HALO = 32
MESH = pl.DeviceIdType.MESH


def exchange_kernel(
    kern_count, tile_count, image_ref, taps_ref, all_taps, above, below,
    tap_send, tap_recv, halo_send, halo_recv, own_sem,
):
    tile = lax.axis_index("tile")
    kern = lax.axis_index("kern")
    rows = image_ref.shape[1]
    up = lax.rem(tile + tile_count - 1, tile_count)
    down = lax.rem(tile + 1, tile_count)
    barrier = pltpu.get_barrier_semaphore()
    for step in range(1, kern_count):
        peer = lax.rem(kern + step, kern_count)
        pl.semaphore_signal(barrier, inc=1, device_id=(tile, peer), device_id_type=MESH)
    for neighbour in (up, down):
        pl.semaphore_signal(barrier, inc=1, device_id=(neighbour, kern), device_id_type=MESH)
    own = pltpu.make_async_copy(taps_ref, all_taps.at[kern], own_sem)
    own.start()
    pl.semaphore_wait(barrier, kern_count - 1 + 2)
    copies = []
    for step in range(1, kern_count):
        peer = lax.rem(kern + step, kern_count)
        copies.append(
            pltpu.make_async_remote_copy(
                src_ref=taps_ref,
                dst_ref=all_taps.at[kern],
                send_sem=tap_send.at[step],
                recv_sem=tap_recv.at[step],
                device_id=(tile, peer),
                device_id_type=MESH,
            )
        )
    copies.append(
        pltpu.make_async_remote_copy(
            src_ref=image_ref.at[:, pl.ds(rows - HALO, HALO), :],
            dst_ref=above,
            send_sem=halo_send.at[0],
            recv_sem=halo_recv.at[0],
            device_id=(down, kern),
            device_id_type=MESH,
        )
    )
    copies.append(
        pltpu.make_async_remote_copy(
            src_ref=image_ref.at[:, pl.ds(0, HALO), :],
            dst_ref=below,
            send_sem=halo_send.at[1],
            recv_sem=halo_recv.at[1],
            device_id=(up, kern),
            device_id_type=MESH,
        )
    )
    for copy in copies:
        copy.start()
    own.wait()
    for copy in copies:
        copy.wait()


def compute_kernel(
    span, share, clip_rows, clip_cols, image_ref, taps_ref, above_ref, below_ref,
    grad_out, resist_out, mask_rows, target_rows, toeplitz, shifted, fields, adjoint, spread,
    resist_rows, grad_rows,
):
    tile = lax.axis_index("tile")
    kern = lax.axis_index("kern")
    rows, width = image_ref.shape[1:]
    margin = (span - 1) // 2
    half = (rows + 2 * margin) // 2
    padded = -(-half // 8) * 8
    source_count = taps_ref.shape[0]
    part_count = 2 * source_count
    depth = taps_ref.shape[2]

    for held, plane in ((mask_rows, 0), (target_rows, 1)):
        keep_above = (tile > 0).astype(jnp.float32)
        keep_below = (tile < lax.axis_size("tile") - 1).astype(jnp.float32)
        held[0:HALO, :] = above_ref[plane].astype(jnp.float32) * keep_above
        held[HALO : HALO + rows, :] = image_ref[plane].astype(jnp.float32)
        held[HALO + rows :, :] = below_ref[plane].astype(jnp.float32) * keep_below

    for source in range(source_count):
        for part in range(2):
            first = (2 * source + part) * padded
            for chunk in range(depth // 128):
                lanes = slice(chunk * 128, (chunk + 1) * 128)
                row = jnp.broadcast_to(taps_ref[source, part : part + 1, lanes], (padded, 128))
                turned = pltpu.roll(row, 0, 1, stride=1, stride_axis=0)
                toeplitz[first : first + padded, lanes] = turned.astype(jnp.bfloat16)

    for block in range(2):
        top = HALO - 2 * margin + block * half
        window = mask_rows[top : top + PITCH, :]
        lanes = slice(block * width, (block + 1) * width)
        for column in range(span):
            turned = window if column == 0 else pltpu.roll(window, width - column, 1)
            shifted[column * PITCH : (column + 1) * PITCH, lanes] = turned.astype(jnp.bfloat16)
        shifted[span * PITCH :, lanes] = jnp.zeros((depth - span * PITCH, width), jnp.bfloat16)

    fields[...] = jnp.dot(toeplitz[...], shifted[...], preferred_element_type=jnp.float32)

    row_at = lax.broadcasted_iota(jnp.int32, (padded, width), 0)
    col_at = lax.broadcasted_iota(jnp.int32, (padded, width), 1)
    clip_col = kern * share - margin + col_at
    col_inside = jnp.logical_and(clip_col >= 0, clip_col < clip_cols)
    for block in range(2):
        lanes = slice(block * width, (block + 1) * width)
        aerial = jnp.zeros((padded, width), jnp.float32)
        for source in range(source_count):
            weight = taps_ref[source, 2:3, 0:width]
            first = 2 * source * padded
            real = fields[first : first + padded, lanes]
            imag = fields[first + padded : first + 2 * padded, lanes]
            aerial = aerial + weight * (real * real + imag * imag)
        resist = 1.0 / (1.0 + jnp.exp(-SLOPE_FACTOR * (aerial - LEVEL_VALUE)))
        resist_rows[block * half : block * half + padded, :] = resist
        top = HALO - margin + block * half
        target = pltpu.roll(target_rows[top : top + padded, :], width - margin, 1)
        sense = 2.0 * (resist - target) * SLOPE_FACTOR * resist * (1.0 - resist)
        clip_row = tile * rows - margin + block * half + row_at
        inside = jnp.logical_and(jnp.logical_and(clip_row >= 0, clip_row < clip_rows), row_at < half)
        sense = jnp.where(jnp.logical_and(inside, col_inside), sense, 0.0)
        for source in range(source_count):
            weight = taps_ref[source, 2:3, 0:width]
            scaled = 2.0 * weight * sense
            for part in range(2):
                first = (2 * source + part) * padded
                adjoint[first : first + padded, lanes] = (
                    scaled * fields[first : first + padded, lanes]
                ).astype(jnp.bfloat16)
    resist_out[...] = pltpu.roll(resist_rows[margin : margin + rows, :], width - margin, 1)[:, :share]

    spread[...] = lax.dot_general(
        toeplitz[...], adjoint[...], (((0,), (0,)), ((), ())), preferred_element_type=jnp.float32
    )

    grads = []
    for block in range(2):
        lanes = slice(block * width, (block + 1) * width)
        total = spread[0:PITCH, lanes]
        for column in range(1, span):
            total = total + pltpu.roll(
                spread[column * PITCH : (column + 1) * PITCH, lanes], column, 1
            )
        grads.append(total)
    grad_rows[...] = jnp.zeros_like(grad_rows)
    grad_rows[0:PITCH, :] = grads[0]
    grad_rows[half : half + PITCH, :] += grads[1]
    grad_out[...] = pltpu.roll(
        grad_rows[2 * margin : 2 * margin + rows, :], width - 2 * margin, 1
    )[:, :share]


def on_device(mask, target, kernels, source_weight, assign):
    rows, col_count = mask.shape
    span = kernels.shape[-1]
    margin = (span - 1) // 2
    kern_count = lax.axis_size("kern")
    tile_count = lax.axis_size("tile")
    share = col_count // kern_count
    kern = lax.axis_index("kern")
    width = -(-(share + 4 * margin) // 128) * 128
    columns = span + span % 2
    depth = columns * PITCH
    half = (rows + 2 * margin) // 2
    padded = -(-half // 8) * 8
    parts = 2 * kern_count

    both = jnp.stack([mask.astype(jnp.bfloat16), target.astype(jnp.bfloat16)])
    both = jnp.pad(both, ((0, 0), (0, 0), (2 * margin, width)))
    image = lax.dynamic_slice_in_dim(both, kern * share, width, 2)
    picked = (assign[0] == jnp.arange(source_weight.shape[0])).astype(jnp.float32)
    weight = jnp.sum(picked * source_weight) / jnp.sum(source_weight)
    taps = jnp.swapaxes(kernels[0].astype(jnp.float32), 1, 2)
    taps = jnp.pad(taps, ((0, 0), (0, columns - span), (0, PITCH - span))).reshape(2, depth)
    taps = jnp.concatenate([taps, jnp.full((1, depth), weight, jnp.float32)])

    in_vmem = pl.BlockSpec(memory_space=pltpu.VMEM)
    all_taps, above, below = pl.pallas_call(
        functools.partial(exchange_kernel, kern_count, tile_count),
        out_shape=(
            jax.ShapeDtypeStruct((kern_count, 3, depth), jnp.float32),
            jax.ShapeDtypeStruct((2, HALO, width), jnp.bfloat16),
            jax.ShapeDtypeStruct((2, HALO, width), jnp.bfloat16),
        ),
        in_specs=[in_vmem] * 2,
        out_specs=(in_vmem,) * 3,
        scratch_shapes=[
            pltpu.SemaphoreType.DMA((kern_count,)),
            pltpu.SemaphoreType.DMA((kern_count,)),
            pltpu.SemaphoreType.DMA((2,)),
            pltpu.SemaphoreType.DMA((2,)),
            pltpu.SemaphoreType.DMA,
        ],
        compiler_params=pltpu.CompilerParams(collective_id=0, has_side_effects=True),
        name="exchange",
    )(image, taps)

    return pl.pallas_call(
        functools.partial(compute_kernel, span, share, rows * tile_count, col_count),
        out_shape=(
            jax.ShapeDtypeStruct((rows, share), jnp.float32),
            jax.ShapeDtypeStruct((rows, share), jnp.float32),
        ),
        in_specs=[in_vmem] * 4,
        out_specs=(in_vmem,) * 2,
        scratch_shapes=[
            pltpu.VMEM((rows + 2 * HALO, width), jnp.float32),
            pltpu.VMEM((rows + 2 * HALO, width), jnp.float32),
            pltpu.VMEM((parts * padded, depth), jnp.bfloat16),
            pltpu.VMEM((depth, 2 * width), jnp.bfloat16),
            pltpu.VMEM((parts * padded, 2 * width), jnp.float32),
            pltpu.VMEM((parts * padded, 2 * width), jnp.bfloat16),
            pltpu.VMEM((depth, 2 * width), jnp.float32),
            pltpu.VMEM((half + padded, width), jnp.float32),
            pltpu.VMEM((half + PITCH, width), jnp.float32),
        ],
        compiler_params=pltpu.CompilerParams(vmem_limit_bytes=56 * 1024 * 1024),
        name="image_gradient",
    )(image, all_taps, above, below)


def solution(mesh):
    placed = (P("tile", None), P("tile", None), P("kern", None, None, None), P(), P("kern"))
    return jax.shard_map(
        on_device,
        mesh=mesh,
        in_specs=placed,
        out_specs=(P("tile", "kern"), P("tile", "kern")),
        check_vma=False,
    )
```

```python
import functools

import jax
import jax.numpy as jnp
from jax import lax
from jax.experimental import pallas as pl
from jax.experimental.pallas import tpu as pltpu
from jax.sharding import PartitionSpec as P

SLOPE_FACTOR = 4.0
LEVEL_VALUE = 0.6
PITCH = 64
MASK_HALO = 32
TARGET_HALO = 16
SEGMENT = 32
MESH = pl.DeviceIdType.MESH
IN_VMEM = pl.BlockSpec(memory_space=pltpu.VMEM)


def slot_of(column):
    if column < 8:
        return 2 * column
    if column < 16:
        return 2 * (column - 8) + 1
    if column < 19:
        return 16 + 2 * (column - 16)
    return 17 + 2 * (column - 19)


def gradient_kernel(
    sizes, mask_hbm, target_hbm, kernel_ref, weight_ref, assign_ref, grad_out, resist_out,
    mask_window, target_window, send_up, send_down, above, below, square, own_taps, all_taps,
    mask_rows, target_rows, toeplitz, shifted, fields, adjoint, spread, resist_rows, grad_rows,
    load_sem, tap_send, tap_recv, halo_send, halo_recv,
):
    kern_count, tile_count, span, share, width = sizes
    tile = lax.axis_index("tile")
    kern = lax.axis_index("kern")
    rows, clip_cols = mask_hbm.shape
    clip_rows = rows * tile_count
    margin = (span - 1) // 2
    half = (rows + 2 * margin) // 2
    padded = -(-half // 8) * 8
    depth = toeplitz.shape[1]
    has_up = tile > 0
    has_down = tile < tile_count - 1

    barrier = pltpu.get_barrier_semaphore()
    for step in range(1, kern_count):
        peer = lax.rem(kern + step, kern_count)
        pl.semaphore_signal(barrier, inc=1, device_id=(tile, peer), device_id_type=MESH)

    @pl.when(has_up)
    def _():
        pl.semaphore_signal(barrier, inc=1, device_id=(tile - 1, kern), device_id_type=MESH)

    @pl.when(has_down)
    def _():
        pl.semaphore_signal(barrier, inc=1, device_id=(tile + 1, kern), device_id_type=MESH)

    start = kern * share - 2 * margin
    loaded = width + 128
    base = (start + 128) // 128 * 128 - 128
    base = jnp.minimum(jnp.maximum(base, 0), clip_cols - loaded)
    base = pl.multiple_of(base, 128)
    loads = [
        pltpu.make_async_copy(mask_hbm.at[:, pl.ds(base, loaded)], mask_window, load_sem.at[0]),
        pltpu.make_async_copy(target_hbm.at[:, pl.ds(base, loaded)], target_window, load_sem.at[1]),
    ]
    for load in loads:
        load.start()

    square[...] = jnp.zeros_like(square)
    for row in range(span):
        pair = kernel_ref[row].astype(jnp.float32)
        square[0, row : row + 1, 0:span] = pair[0:1]
        square[1, row : row + 1, 0:span] = pair[1:2]
    lane = lax.broadcasted_iota(jnp.int32, (8, 128), 1)
    packed = []
    for part in range(2):
        turned = square[part].T
        block = turned[0:8]
        block = block + pltpu.roll(turned[8:16], SEGMENT, 1)
        block = block + pltpu.roll(turned[16:24], 2 * SEGMENT, 1)
        packed.append(jnp.where(lane < 3 * SEGMENT, block, assign_ref[0].astype(jnp.float32)))
    own_taps[...] = jnp.concatenate(packed).astype(jnp.bfloat16)

    for load in loads:
        load.wait()
    clip_col = start + lax.broadcasted_iota(jnp.int32, (rows, width), 1)
    col_inside = jnp.logical_and(clip_col >= 0, clip_col < clip_cols)
    back = lax.rem(base - start + loaded, loaded)
    mask_own = pltpu.roll(mask_window[...], back, 1)[:, :width]
    mask_own = jnp.where(col_inside, mask_own, 0.0).astype(jnp.bfloat16)
    target_own = pltpu.roll(target_window[...].astype(jnp.float32), back, 1)[:, :width]
    target_own = target_own.astype(jnp.bfloat16)
    send_up[0:MASK_HALO, :] = mask_own[0:MASK_HALO]
    send_up[MASK_HALO:, :] = target_own[0:TARGET_HALO]
    send_down[0:MASK_HALO, :] = mask_own[rows - MASK_HALO :]
    send_down[MASK_HALO:, :] = target_own[rows - TARGET_HALO :]

    pl.semaphore_wait(barrier, kern_count - 1 + has_up.astype(jnp.int32) + has_down.astype(jnp.int32))
    tap_copies = []
    for step in range(1, kern_count):
        peer = lax.rem(kern + step, kern_count)
        tap_copies.append(
            pltpu.make_async_remote_copy(
                src_ref=own_taps,
                dst_ref=all_taps.at[kern],
                send_sem=tap_send.at[step],
                recv_sem=tap_recv.at[step],
                device_id=(tile, peer),
                device_id_type=MESH,
            )
        )
    upward = pltpu.make_async_remote_copy(
        src_ref=send_up,
        dst_ref=below,
        send_sem=halo_send.at[0],
        recv_sem=halo_recv.at[0],
        device_id=(tile - 1, kern),
        device_id_type=MESH,
    )
    downward = pltpu.make_async_remote_copy(
        src_ref=send_down,
        dst_ref=above,
        send_sem=halo_send.at[1],
        recv_sem=halo_recv.at[1],
        device_id=(tile + 1, kern),
        device_id_type=MESH,
    )
    pl.when(has_up)(upward.start)
    pl.when(has_down)(downward.start)
    for copy in tap_copies:
        copy.start()
    all_taps[kern] = own_taps[...]

    mask_rows[MASK_HALO : MASK_HALO + rows, :] = mask_own.astype(jnp.float32)
    target_rows[TARGET_HALO : TARGET_HALO + rows, :] = target_own.astype(jnp.float32)

    @pl.when(has_up)
    def _():
        downward.wait_recv()

    @pl.when(jnp.logical_not(has_up))
    def _():
        above[...] = jnp.zeros_like(above)

    @pl.when(has_down)
    def _():
        upward.wait_recv()

    @pl.when(jnp.logical_not(has_down))
    def _():
        below[...] = jnp.zeros_like(below)

    mask_rows[0:MASK_HALO, :] = above[0:MASK_HALO, :].astype(jnp.float32)
    mask_rows[MASK_HALO + rows :, :] = below[0:MASK_HALO, :].astype(jnp.float32)
    target_rows[0:TARGET_HALO, :] = above[MASK_HALO:, :].astype(jnp.float32)
    target_rows[TARGET_HALO + rows :, :] = below[MASK_HALO:, :].astype(jnp.float32)

    for block in range(2):
        top = MASK_HALO - 2 * margin + block * half
        window = mask_rows[top : top + PITCH, :]
        lanes = slice(block * width, (block + 1) * width)
        for column in range(span):
            turned = window if column == 0 else pltpu.roll(window, width - column, 1)
            place = slot_of(column) * PITCH
            shifted[place : place + PITCH, lanes] = turned.astype(jnp.bfloat16)
        shifted[span * PITCH :, lanes] = jnp.zeros((depth - span * PITCH, width), jnp.bfloat16)

    for copy in tap_copies:
        copy.wait_recv()
    weights = weight_ref[...]
    total = jnp.sum(weights, axis=1, keepdims=True)
    slot_ids = lax.broadcasted_iota(jnp.int32, weights.shape, 1).astype(jnp.float32)
    first_part = lane < SEGMENT
    second_part = jnp.logical_and(lane >= 2 * SEGMENT, lane < 3 * SEGMENT)
    shares = []
    for source in range(kern_count):
        block = all_taps[source].astype(jnp.float32)
        picked = jnp.where(slot_ids == block[0:1, 3 * SEGMENT : 3 * SEGMENT + 1], weights, 0.0)
        shares.append(jnp.sum(picked, axis=1, keepdims=True) / total)
        for part in range(2):
            taps = block[8 * part : 8 * part + 8]
            near = jnp.where(
                first_part, taps, jnp.where(second_part, pltpu.roll(taps, SEGMENT, 1), 0.0)
            )
            far = jnp.where(first_part, pltpu.roll(taps, 2 * SEGMENT, 1), 0.0)
            last = jnp.where(second_part, taps, 0.0)
            first = (2 * source + part) * padded
            for chunk in range(depth // 128):
                if chunk < 8:
                    row = near[chunk : chunk + 1]
                else:
                    row = far[chunk - 8 : chunk - 7] + last[chunk - 5 : chunk - 4]
                row = jnp.broadcast_to(row, (padded, 128))
                turned = pltpu.roll(row, 0, 1, stride=1, stride_axis=0)
                lanes = slice(chunk * 128, (chunk + 1) * 128)
                toeplitz[first : first + padded, lanes] = turned.astype(jnp.bfloat16)

    fields[...] = jnp.dot(toeplitz[...], shifted[...], preferred_element_type=jnp.float32)

    row_at = lax.broadcasted_iota(jnp.int32, (padded, width), 0)
    col_at = lax.broadcasted_iota(jnp.int32, (padded, width), 1)
    clip_col = kern * share - margin + col_at
    col_inside = jnp.logical_and(clip_col >= 0, clip_col < clip_cols)
    for block in range(2):
        lanes = slice(block * width, (block + 1) * width)
        aerial = jnp.zeros((padded, width), jnp.float32)
        for source in range(kern_count):
            first = 2 * source * padded
            real = fields[first : first + padded, lanes]
            imag = fields[first + padded : first + 2 * padded, lanes]
            aerial = aerial + shares[source] * (real * real + imag * imag)
        resist = 1.0 / (1.0 + jnp.exp(-SLOPE_FACTOR * (aerial - LEVEL_VALUE)))
        resist_rows[block * half : block * half + padded, :] = resist
        top = TARGET_HALO - margin + block * half
        target = pltpu.roll(target_rows[top : top + padded, :], width - margin, 1)
        sense = 2.0 * (resist - target) * SLOPE_FACTOR * resist * (1.0 - resist)
        clip_row = tile * rows - margin + block * half + row_at
        inside = jnp.logical_and(jnp.logical_and(clip_row >= 0, clip_row < clip_rows), row_at < half)
        sense = jnp.where(jnp.logical_and(inside, col_inside), sense, 0.0)
        for source in range(kern_count):
            scaled = (2.0 * shares[source]) * sense
            for part in range(2):
                first = (2 * source + part) * padded
                adjoint[first : first + padded, lanes] = (
                    scaled * fields[first : first + padded, lanes]
                ).astype(jnp.bfloat16)
    resist_out[...] = pltpu.roll(resist_rows[margin : margin + rows, :], width - margin, 1)[:, :share]

    spread[...] = lax.dot_general(
        toeplitz[...], adjoint[...], (((0,), (0,)), ((), ())), preferred_element_type=jnp.float32
    )

    grads = []
    for block in range(2):
        lanes = slice(block * width, (block + 1) * width)
        gathered = spread[0:PITCH, lanes]
        for column in range(1, span):
            place = slot_of(column) * PITCH
            gathered = gathered + pltpu.roll(spread[place : place + PITCH, lanes], column, 1)
        grads.append(gathered)
    grad_rows[...] = jnp.zeros_like(grad_rows)
    grad_rows[0:PITCH, :] = grads[0]
    grad_rows[half : half + PITCH, :] += grads[1]
    grad_out[...] = pltpu.roll(
        grad_rows[2 * margin : 2 * margin + rows, :], width - 2 * margin, 1
    )[:, :share]

    for copy in tap_copies:
        copy.wait_send()
    pl.when(has_up)(upward.wait_send)
    pl.when(has_down)(downward.wait_send)


def on_device(mask, target, kernels, source_weight, assign):
    rows, col_count = mask.shape
    span = kernels.shape[-1]
    margin = (span - 1) // 2
    kern_count = lax.axis_size("kern")
    tile_count = lax.axis_size("tile")
    share = col_count // kern_count
    width = -(-(share + 4 * margin) // 128) * 128
    depth = (span + span % 2) * PITCH
    half = (rows + 2 * margin) // 2
    padded = -(-half // 8) * 8
    parts = 2 * kern_count
    halo = MASK_HALO + TARGET_HALO
    in_hbm = pl.BlockSpec(memory_space=pl.ANY)
    return pl.pallas_call(
        functools.partial(gradient_kernel, (kern_count, tile_count, span, share, width)),
        out_shape=(
            jax.ShapeDtypeStruct((rows, share), jnp.float32),
            jax.ShapeDtypeStruct((rows, share), jnp.float32),
        ),
        in_specs=[in_hbm, in_hbm, IN_VMEM, IN_VMEM, pl.BlockSpec(memory_space=pltpu.SMEM)],
        out_specs=(IN_VMEM, IN_VMEM),
        scratch_shapes=[
            pltpu.VMEM((rows, width + 128), jnp.float32),
            pltpu.VMEM((rows, width + 128), jnp.int32),
            pltpu.VMEM((halo, width), jnp.bfloat16),
            pltpu.VMEM((halo, width), jnp.bfloat16),
            pltpu.VMEM((halo, width), jnp.bfloat16),
            pltpu.VMEM((halo, width), jnp.bfloat16),
            pltpu.VMEM((2, 128, 128), jnp.float32),
            pltpu.VMEM((16, 128), jnp.bfloat16),
            pltpu.VMEM((kern_count, 16, 128), jnp.bfloat16),
            pltpu.VMEM((rows + 2 * MASK_HALO, width), jnp.float32),
            pltpu.VMEM((rows + 2 * TARGET_HALO, width), jnp.float32),
            pltpu.VMEM((parts * padded, depth), jnp.bfloat16),
            pltpu.VMEM((depth, 2 * width), jnp.bfloat16),
            pltpu.VMEM((parts * padded, 2 * width), jnp.float32),
            pltpu.VMEM((parts * padded, 2 * width), jnp.bfloat16),
            pltpu.VMEM((depth, 2 * width), jnp.float32),
            pltpu.VMEM((half + padded, width), jnp.float32),
            pltpu.VMEM((half + PITCH, width), jnp.float32),
            pltpu.SemaphoreType.DMA((2,)),
            pltpu.SemaphoreType.DMA((kern_count,)),
            pltpu.SemaphoreType.DMA((kern_count,)),
            pltpu.SemaphoreType.DMA((2,)),
            pltpu.SemaphoreType.DMA((2,)),
        ],
        compiler_params=pltpu.CompilerParams(
            collective_id=0, has_side_effects=True, vmem_limit_bytes=56 * 1024 * 1024
        ),
        name="image_gradient",
    )(mask, target, jnp.swapaxes(kernels[0], 0, 1), source_weight[None, :], assign)


def solution(mesh):
    placed = (P("tile", None), P("tile", None), P("kern", None, None, None), P(), P("kern"))
    return jax.shard_map(
        on_device,
        mesh=mesh,
        in_specs=placed,
        out_specs=(P("tile", "kern"), P("tile", "kern")),
        check_vma=False,
    )
```

```python
import functools

import jax
import jax.numpy as jnp
from jax import lax
from jax.experimental import pallas as pl
from jax.experimental.pallas import tpu as pltpu
from jax.sharding import PartitionSpec as P

SLOPE_FACTOR = 4.0
LEVEL_VALUE = 0.6
BLOCKS = 3
PITCH = 48
MASK_HALO = 32
TARGET_HALO = 16
MESH = pl.DeviceIdType.MESH
IN_VMEM = pl.BlockSpec(memory_space=pltpu.VMEM)
IN_ANY = pl.BlockSpec(memory_space=pl.ANY)


def gradient_kernel(
    sizes, mask_hbm, target_hbm, kernel_ref, weight_ref, assign_hbm, grad_out, resist_out,
    mask_window, target_window, send_up, send_down, above, below, square, tap_rows, own_taps,
    all_taps, mask_rows, target_rows, toeplitz, shifted, fields, adjoint, spread, resist_rows,
    grad_rows, resist_own, grad_own, assign_own, load_sem, store_sem, tap_send, tap_recv, halo_send, halo_recv,
):
    kern_count, tile_count, span, share, width = sizes
    tile = lax.axis_index("tile")
    kern = lax.axis_index("kern")
    rows, clip_cols = mask_hbm.shape
    clip_rows = rows * tile_count
    margin = (span - 1) // 2
    height = (rows + 2 * margin) // BLOCKS
    padded = -(-height // 16) * 16
    depth = toeplitz.shape[1]
    reach = share + 4 * margin
    lanes = shifted.shape[1]
    has_up = tile > 0
    has_down = tile < tile_count - 1

    barrier = pltpu.get_barrier_semaphore()
    for step in range(1, kern_count):
        peer = lax.rem(kern + step, kern_count)
        pl.semaphore_signal(barrier, inc=1, device_id=(tile, peer), device_id_type=MESH)

    @pl.when(has_up)
    def _():
        pl.semaphore_signal(barrier, inc=1, device_id=(tile - 1, kern), device_id_type=MESH)

    @pl.when(has_down)
    def _():
        pl.semaphore_signal(barrier, inc=1, device_id=(tile + 1, kern), device_id_type=MESH)

    start = kern * share - 2 * margin
    loaded = width + 128
    base = (start + 128) // 128 * 128 - 128
    base = jnp.minimum(jnp.maximum(base, 0), clip_cols - loaded)
    base = pl.multiple_of(base, 128)
    assign_load = pltpu.make_async_copy(assign_hbm, assign_own, load_sem.at[2])
    assign_load.start()
    loads = [
        pltpu.make_async_copy(mask_hbm.at[:, pl.ds(base, loaded)], mask_window, load_sem.at[0]),
        pltpu.make_async_copy(target_hbm.at[:, pl.ds(base, loaded)], target_window, load_sem.at[1]),
    ]
    for load in loads:
        load.start()

    square[...] = jnp.zeros_like(square)
    for row in range(span):
        pair = kernel_ref[row].astype(jnp.float32)
        square[0, row : row + 1, 0:span] = pair[0:1]
        square[1, row : row + 1, 0:span] = pair[1:2]
    assign_load.wait()
    lane = lax.broadcasted_iota(jnp.int32, (1, 128), 1)
    chunk_count = depth // 128
    for part in range(2):
        turned = square[part].T
        chunks = [jnp.zeros((1, 128), jnp.float32)] * chunk_count
        for column in range(span):
            chunk, offset = divmod(column * PITCH, 128)
            row = turned[column : column + 1]
            row = pltpu.roll(row, offset, 1) if offset else row
            if offset + span <= 128:
                chunks[chunk] = chunks[chunk] + row
            else:
                chunks[chunk] = chunks[chunk] + jnp.where(lane >= offset, row, 0.0)
                chunks[chunk + 1] = chunks[chunk + 1] + jnp.where(lane < offset, row, 0.0)
        mark = assign_own[0].astype(jnp.float32)
        chunks[-1] = jnp.where(lane >= 112, mark, chunks[-1])
        for chunk in range(chunk_count):
            tap_rows[8 * part + chunk : 8 * part + chunk + 1, :] = chunks[chunk]
    own_taps[...] = tap_rows[...].astype(jnp.bfloat16)

    pl.semaphore_wait(barrier, kern_count - 1 + has_up.astype(jnp.int32) + has_down.astype(jnp.int32))
    tap_copies = []
    for step in range(1, kern_count):
        peer = lax.rem(kern + step, kern_count)
        tap_copies.append(
            pltpu.make_async_remote_copy(
                src_ref=own_taps,
                dst_ref=all_taps.at[step],
                send_sem=tap_send.at[step],
                recv_sem=tap_recv.at[step],
                device_id=(tile, peer),
                device_id_type=MESH,
            )
        )
    for copy in tap_copies:
        copy.start()

    for load in loads:
        load.wait()
    clip_col = start + lax.broadcasted_iota(jnp.int32, (rows, width), 1)
    col_inside = jnp.logical_and(clip_col >= 0, clip_col < clip_cols)
    back = lax.rem(base - start + loaded, loaded)
    mask_own = pltpu.roll(mask_window[...], back, 1)[:, :width]
    mask_own = jnp.where(col_inside, mask_own, 0.0).astype(jnp.bfloat16)
    target_own = pltpu.roll(target_window[...].astype(jnp.float32), back, 1)[:, :width]
    target_own = target_own.astype(jnp.bfloat16)
    send_up[0:MASK_HALO, :] = mask_own[0:MASK_HALO]
    send_up[MASK_HALO:, :] = target_own[0:TARGET_HALO]
    send_down[0:MASK_HALO, :] = mask_own[rows - MASK_HALO :]
    send_down[MASK_HALO:, :] = target_own[rows - TARGET_HALO :]
    upward = pltpu.make_async_remote_copy(
        src_ref=send_up,
        dst_ref=below,
        send_sem=halo_send.at[0],
        recv_sem=halo_recv.at[0],
        device_id=(tile - 1, kern),
        device_id_type=MESH,
    )
    downward = pltpu.make_async_remote_copy(
        src_ref=send_down,
        dst_ref=above,
        send_sem=halo_send.at[1],
        recv_sem=halo_recv.at[1],
        device_id=(tile + 1, kern),
        device_id_type=MESH,
    )
    pl.when(has_up)(upward.start)
    pl.when(has_down)(downward.start)
    mask_rows[MASK_HALO : MASK_HALO + rows, :] = mask_own.astype(jnp.float32)
    target_rows[TARGET_HALO : TARGET_HALO + rows, :] = target_own.astype(jnp.float32)

    weights = weight_ref[...]
    total = jnp.sum(weights, axis=1, keepdims=True)
    slot_ids = lax.broadcasted_iota(jnp.int32, weights.shape, 1).astype(jnp.float32)
    own_lane = lax.broadcasted_iota(jnp.int32, (padded, 128), 1)
    own_row = lax.broadcasted_iota(jnp.int32, (padded, 128), 0)
    same_chunk = own_lane >= own_row
    shares = []
    for source in range(kern_count):
        if source == 0:
            block = own_taps[...].astype(jnp.float32)
        else:
            tap_copies[source - 1].wait_recv()
            block = all_taps[source].astype(jnp.float32)
        picked = jnp.where(slot_ids == block[7:8, 112:113], weights, 0.0)
        shares.append(jnp.sum(picked, axis=1, keepdims=True) / total)
        for part in range(2):
            first = (2 * source + part) * padded
            before = jnp.zeros((padded, 128), jnp.float32)
            for chunk in range(chunk_count):
                at = 8 * part + chunk
                row = jnp.broadcast_to(block[at : at + 1], (padded, 128))
                turned = pltpu.roll(row, 0, 1, stride=1, stride_axis=0)
                toeplitz[first : first + padded, chunk * 128 : (chunk + 1) * 128] = jnp.where(
                    same_chunk, turned, before
                ).astype(jnp.bfloat16)
                before = turned

    @pl.when(has_up)
    def _():
        downward.wait_recv()

    @pl.when(jnp.logical_not(has_up))
    def _():
        above[...] = jnp.zeros_like(above)

    @pl.when(has_down)
    def _():
        upward.wait_recv()

    @pl.when(jnp.logical_not(has_down))
    def _():
        below[...] = jnp.zeros_like(below)

    mask_rows[0:MASK_HALO, :] = above[0:MASK_HALO, :].astype(jnp.float32)
    mask_rows[MASK_HALO + rows :, :] = below[0:MASK_HALO, :].astype(jnp.float32)
    target_rows[0:TARGET_HALO, :] = above[MASK_HALO:, :].astype(jnp.float32)
    target_rows[TARGET_HALO + rows :, :] = below[MASK_HALO:, :].astype(jnp.float32)

    def side_by_side(held, top, count, shift):
        pieces = []
        for block in range(BLOCKS):
            piece = held[top + block * height : top + block * height + count, :]
            piece = pltpu.roll(piece, width - shift, 1) if shift else piece
            pieces.append(piece[:, :reach])
        if lanes > BLOCKS * reach:
            pieces.append(jnp.zeros((count, lanes - BLOCKS * reach), jnp.float32))
        return jnp.concatenate(pieces, axis=1)

    window = side_by_side(mask_rows, MASK_HALO - 2 * margin, PITCH, 0)
    for column in range(span):
        turned = window if column == 0 else pltpu.roll(window, lanes - column, 1)
        shifted[column * PITCH : (column + 1) * PITCH, :] = turned.astype(jnp.bfloat16)
    shifted[span * PITCH :, :] = jnp.zeros((depth - span * PITCH, lanes), jnp.bfloat16)

    fields[...] = jnp.dot(toeplitz[...], shifted[...], preferred_element_type=jnp.float32)

    row_at = lax.broadcasted_iota(jnp.int32, (padded, lanes), 0)
    col_at = lax.broadcasted_iota(jnp.int32, (padded, lanes), 1)
    clip_row = tile * rows - margin + row_at
    clip_col = kern * share - margin + col_at
    for block in range(1, BLOCKS):
        later = col_at >= block * reach
        clip_row = jnp.where(later, clip_row + height, clip_row)
        clip_col = jnp.where(later, clip_col - reach, clip_col)
    inside = jnp.logical_and(
        jnp.logical_and(clip_row >= 0, clip_row < clip_rows),
        jnp.logical_and(clip_col >= 0, clip_col < clip_cols),
    )
    inside = jnp.logical_and(inside, row_at < height)
    target = side_by_side(target_rows, TARGET_HALO - margin, padded, margin)
    aerial = jnp.zeros((padded, lanes), jnp.float32)
    for source in range(kern_count):
        first = 2 * source * padded
        real = fields[first : first + padded, :]
        imag = fields[first + padded : first + 2 * padded, :]
        aerial = aerial + shares[source] * (real * real + imag * imag)
    resist = 1.0 / (1.0 + jnp.exp(-SLOPE_FACTOR * (aerial - LEVEL_VALUE)))
    sense = 2.0 * (resist - target) * SLOPE_FACTOR * resist * (1.0 - resist)
    sense = jnp.where(inside, sense, 0.0)
    for source in range(kern_count):
        scaled = (2.0 * shares[source]) * sense
        for part in range(2):
            first = (2 * source + part) * padded
            adjoint[first : first + padded, :] = (
                scaled * fields[first : first + padded, :]
            ).astype(jnp.bfloat16)
    for block in range(BLOCKS):
        piece = pltpu.roll(resist, lanes - block * reach - margin, 1)[:, :share]
        resist_rows[block * height : block * height + padded, :] = piece
    resist_own[...] = resist_rows[margin : margin + rows, :]
    resist_store = pltpu.make_async_copy(resist_own, resist_out, store_sem.at[0])
    resist_store.start()

    spread[...] = lax.dot_general(
        toeplitz[...], adjoint[...], (((0,), (0,)), ((), ())), preferred_element_type=jnp.float32
    )

    gathered = spread[0:PITCH, :]
    for column in range(1, span):
        place = column * PITCH
        gathered = gathered + pltpu.roll(spread[place : place + PITCH, :], column, 1)
    grad_rows[...] = jnp.zeros_like(grad_rows)
    for block in range(BLOCKS):
        piece = pltpu.roll(gathered, lanes - block * reach - 2 * margin, 1)[:, :share]
        grad_rows[block * height : block * height + PITCH, :] += piece
    grad_own[...] = grad_rows[2 * margin : 2 * margin + rows, :]
    grad_store = pltpu.make_async_copy(grad_own, grad_out, store_sem.at[1])
    grad_store.start()

    for copy in tap_copies:
        copy.wait_send()
    pl.when(has_up)(upward.wait_send)
    pl.when(has_down)(downward.wait_send)
    resist_store.wait()
    grad_store.wait()


def hand_over_kernel(grad_in, resist_in, grad_out, resist_out, sems):
    moves = [
        pltpu.make_async_copy(grad_in, grad_out, sems.at[0]),
        pltpu.make_async_copy(resist_in, resist_out, sems.at[1]),
    ]
    for move in moves:
        move.start()
    for move in moves:
        move.wait()


def on_device(mask, target, kernels, source_weight, assign):
    rows, col_count = mask.shape
    span = kernels.shape[-1]
    margin = (span - 1) // 2
    kern_count = lax.axis_size("kern")
    tile_count = lax.axis_size("tile")
    share = col_count // kern_count
    reach = share + 4 * margin
    width = -(-reach // 128) * 128
    lanes = -(-BLOCKS * reach // 128) * 128
    depth = -(-span * PITCH // 128) * 128
    height = (rows + 2 * margin) // BLOCKS
    padded = -(-height // 16) * 16
    parts = 2 * kern_count
    halo = MASK_HALO + TARGET_HALO
    image = jax.ShapeDtypeStruct((rows, share), jnp.float32)
    images = pl.pallas_call(
        functools.partial(gradient_kernel, (kern_count, tile_count, span, share, width)),
        out_shape=(image, image),
        in_specs=[IN_ANY, IN_ANY, IN_VMEM, IN_VMEM, IN_ANY],
        out_specs=(IN_ANY, IN_ANY),
        scratch_shapes=[
            pltpu.VMEM((rows, width + 128), jnp.float32),
            pltpu.VMEM((rows, width + 128), jnp.int32),
            pltpu.VMEM((halo, width), jnp.bfloat16),
            pltpu.VMEM((halo, width), jnp.bfloat16),
            pltpu.VMEM((halo, width), jnp.bfloat16),
            pltpu.VMEM((halo, width), jnp.bfloat16),
            pltpu.VMEM((2, 128, 128), jnp.float32),
            pltpu.VMEM((16, 128), jnp.float32),
            pltpu.VMEM((16, 128), jnp.bfloat16),
            pltpu.VMEM((kern_count, 16, 128), jnp.bfloat16),
            pltpu.VMEM((rows + 2 * MASK_HALO, width), jnp.float32),
            pltpu.VMEM((rows + 2 * TARGET_HALO, width), jnp.float32),
            pltpu.VMEM((parts * padded, depth), jnp.bfloat16),
            pltpu.VMEM((depth, lanes), jnp.bfloat16),
            pltpu.VMEM((parts * padded, lanes), jnp.float32),
            pltpu.VMEM((parts * padded, lanes), jnp.bfloat16),
            pltpu.VMEM((depth, lanes), jnp.float32),
            pltpu.VMEM(((BLOCKS - 1) * height + padded, share), jnp.float32),
            pltpu.VMEM(((BLOCKS - 1) * height + PITCH, share), jnp.float32),
            pltpu.VMEM((rows, share), jnp.float32),
            pltpu.VMEM((rows, share), jnp.float32),
            pltpu.SMEM((1,), jnp.int32),
            pltpu.SemaphoreType.DMA((3,)),
            pltpu.SemaphoreType.DMA((2,)),
            pltpu.SemaphoreType.DMA((kern_count,)),
            pltpu.SemaphoreType.DMA((kern_count,)),
            pltpu.SemaphoreType.DMA((2,)),
            pltpu.SemaphoreType.DMA((2,)),
        ],
        compiler_params=pltpu.CompilerParams(
            collective_id=0, has_side_effects=True, vmem_limit_bytes=56 * 1024 * 1024
        ),
        name="image_gradient",
    )(mask, target, jnp.swapaxes(kernels[0], 0, 1), source_weight[None, :], assign)
    return pl.pallas_call(
        hand_over_kernel,
        out_shape=(image, image),
        in_specs=[IN_ANY, IN_ANY],
        out_specs=(IN_ANY, IN_ANY),
        scratch_shapes=[pltpu.SemaphoreType.DMA((2,))],
        compiler_params=pltpu.CompilerParams(vmem_limit_bytes=56 * 1024 * 1024),
        name="hand_over",
    )(*images)


def solution(mesh):
    placed = (P("tile", None), P("tile", None), P("kern", None, None, None), P(), P("kern"))
    return jax.shard_map(
        on_device,
        mesh=mesh,
        in_specs=placed,
        out_specs=(P("tile", "kern"), P("tile", "kern")),
        check_vma=False,
    )
```

```python
import functools

import jax
import jax.numpy as jnp
from jax import lax
from jax.experimental import pallas as pl
from jax.experimental.pallas import tpu as pltpu
from jax.sharding import PartitionSpec as P

SLOPE_FACTOR = 4.0
LEVEL_VALUE = 0.6
BLOCKS = 3
PITCH = 48
MASK_HALO = 32
TARGET_HALO = 16
MESH = pl.DeviceIdType.MESH
IN_VMEM = pl.BlockSpec(memory_space=pltpu.VMEM)
IN_ANY = pl.BlockSpec(memory_space=pl.ANY)


def gradient_kernel(
    sizes, mask_hbm, target_hbm, kernel_hbm, weight_hbm, assign_hbm, grad_out, resist_out,
    mask_window, target_window, send_up, send_down, above, below, square, tap_rows, own_taps,
    all_taps, mask_rows, target_rows, toeplitz, shifted, fields, adjoint, spread, resist_rows,
    grad_rows, resist_own, grad_own, kernel_ref, weight_ref, assign_own, load_sem, store_sem, tap_send, tap_recv, halo_send, halo_recv,
):
    kern_count, tile_count, span, share, width = sizes
    tile = lax.axis_index("tile")
    kern = lax.axis_index("kern")
    rows, clip_cols = mask_hbm.shape
    clip_rows = rows * tile_count
    margin = (span - 1) // 2
    height = (rows + 2 * margin) // BLOCKS
    padded = -(-height // 16) * 16
    depth = toeplitz.shape[1]
    reach = share + 4 * margin
    lanes = shifted.shape[1]
    has_up = tile > 0
    has_down = tile < tile_count - 1

    barrier = pltpu.get_barrier_semaphore()
    for step in range(1, kern_count):
        peer = lax.rem(kern + step, kern_count)
        pl.semaphore_signal(barrier, inc=1, device_id=(tile, peer), device_id_type=MESH)

    @pl.when(has_up)
    def _():
        pl.semaphore_signal(barrier, inc=1, device_id=(tile - 1, kern), device_id_type=MESH)

    @pl.when(has_down)
    def _():
        pl.semaphore_signal(barrier, inc=1, device_id=(tile + 1, kern), device_id_type=MESH)

    start = kern * share - 2 * margin
    loaded = width + 128
    base = (start + 128) // 128 * 128 - 128
    base = jnp.minimum(jnp.maximum(base, 0), clip_cols - loaded)
    base = pl.multiple_of(base, 128)
    small_loads = [
        pltpu.make_async_copy(kernel_hbm, kernel_ref, load_sem.at[2]),
        pltpu.make_async_copy(weight_hbm, weight_ref, load_sem.at[3]),
        pltpu.make_async_copy(assign_hbm, assign_own, load_sem.at[4]),
    ]
    for load in small_loads:
        load.start()
    loads = [
        pltpu.make_async_copy(mask_hbm.at[:, pl.ds(base, loaded)], mask_window, load_sem.at[0]),
        pltpu.make_async_copy(target_hbm.at[:, pl.ds(base, loaded)], target_window, load_sem.at[1]),
    ]
    for load in loads:
        load.start()

    square[...] = jnp.zeros_like(square)
    for load in small_loads:
        load.wait()
    for row in range(span):
        pair = kernel_ref[row].astype(jnp.float32)
        square[0, row : row + 1, 0:span] = pair[0:1]
        square[1, row : row + 1, 0:span] = pair[1:2]
    lane = lax.broadcasted_iota(jnp.int32, (1, 128), 1)
    chunk_count = depth // 128
    for part in range(2):
        turned = square[part].T
        chunks = [jnp.zeros((1, 128), jnp.float32)] * chunk_count
        for column in range(span):
            chunk, offset = divmod(column * PITCH, 128)
            row = turned[column : column + 1]
            row = pltpu.roll(row, offset, 1) if offset else row
            if offset + span <= 128:
                chunks[chunk] = chunks[chunk] + row
            else:
                chunks[chunk] = chunks[chunk] + jnp.where(lane >= offset, row, 0.0)
                chunks[chunk + 1] = chunks[chunk + 1] + jnp.where(lane < offset, row, 0.0)
        mark = assign_own[0].astype(jnp.float32)
        chunks[-1] = jnp.where(lane >= 112, mark, chunks[-1])
        for chunk in range(chunk_count):
            tap_rows[8 * part + chunk : 8 * part + chunk + 1, :] = chunks[chunk]
    own_taps[...] = tap_rows[...].astype(jnp.bfloat16)

    for load in loads:
        load.wait()
    clip_col = start + lax.broadcasted_iota(jnp.int32, (rows, width), 1)
    col_inside = jnp.logical_and(clip_col >= 0, clip_col < clip_cols)
    back = lax.rem(base - start + loaded, loaded)
    mask_own = pltpu.roll(mask_window[...], back, 1)[:, :width]
    mask_own = jnp.where(col_inside, mask_own, 0.0).astype(jnp.bfloat16)
    target_own = pltpu.roll(target_window[...].astype(jnp.float32), back, 1)[:, :width]
    target_own = target_own.astype(jnp.bfloat16)
    send_up[0:MASK_HALO, :] = mask_own[0:MASK_HALO]
    send_up[MASK_HALO:, :] = target_own[0:TARGET_HALO]
    send_down[0:MASK_HALO, :] = mask_own[rows - MASK_HALO :]
    send_down[MASK_HALO:, :] = target_own[rows - TARGET_HALO :]
    upward = pltpu.make_async_remote_copy(
        src_ref=send_up,
        dst_ref=below,
        send_sem=halo_send.at[0],
        recv_sem=halo_recv.at[0],
        device_id=(tile - 1, kern),
        device_id_type=MESH,
    )
    downward = pltpu.make_async_remote_copy(
        src_ref=send_down,
        dst_ref=above,
        send_sem=halo_send.at[1],
        recv_sem=halo_recv.at[1],
        device_id=(tile + 1, kern),
        device_id_type=MESH,
    )
    pl.semaphore_wait(barrier, kern_count - 1 + has_up.astype(jnp.int32) + has_down.astype(jnp.int32))
    tap_copies = []
    for step in range(1, kern_count):
        peer = lax.rem(kern + step, kern_count)
        tap_copies.append(
            pltpu.make_async_remote_copy(
                src_ref=own_taps,
                dst_ref=all_taps.at[step],
                send_sem=tap_send.at[step],
                recv_sem=tap_recv.at[step],
                device_id=(tile, peer),
                device_id_type=MESH,
            )
        )
    for copy in tap_copies:
        copy.start()
    pl.when(has_up)(upward.start)
    pl.when(has_down)(downward.start)
    mask_rows[MASK_HALO : MASK_HALO + rows, :] = mask_own.astype(jnp.float32)
    target_rows[TARGET_HALO : TARGET_HALO + rows, :] = target_own.astype(jnp.float32)

    @pl.when(has_up)
    def _():
        downward.wait_recv()

    @pl.when(jnp.logical_not(has_up))
    def _():
        above[...] = jnp.zeros_like(above)

    @pl.when(has_down)
    def _():
        upward.wait_recv()

    @pl.when(jnp.logical_not(has_down))
    def _():
        below[...] = jnp.zeros_like(below)

    mask_rows[0:MASK_HALO, :] = above[0:MASK_HALO, :].astype(jnp.float32)
    mask_rows[MASK_HALO + rows :, :] = below[0:MASK_HALO, :].astype(jnp.float32)
    target_rows[0:TARGET_HALO, :] = above[MASK_HALO:, :].astype(jnp.float32)
    target_rows[TARGET_HALO + rows :, :] = below[MASK_HALO:, :].astype(jnp.float32)

    def side_by_side(held, top, count, shift):
        pieces = []
        for block in range(BLOCKS):
            piece = held[top + block * height : top + block * height + count, :]
            piece = pltpu.roll(piece, width - shift, 1) if shift else piece
            pieces.append(piece[:, :reach])
        if lanes > BLOCKS * reach:
            pieces.append(jnp.zeros((count, lanes - BLOCKS * reach), jnp.float32))
        return jnp.concatenate(pieces, axis=1)

    window = side_by_side(mask_rows, MASK_HALO - 2 * margin, PITCH, 0)
    for column in range(span):
        turned = window if column == 0 else pltpu.roll(window, lanes - column, 1)
        shifted[column * PITCH : (column + 1) * PITCH, :] = turned.astype(jnp.bfloat16)
    shifted[span * PITCH :, :] = jnp.zeros((depth - span * PITCH, lanes), jnp.bfloat16)

    weights = weight_ref[...]
    total = jnp.sum(weights, axis=1, keepdims=True)
    slot_ids = lax.broadcasted_iota(jnp.int32, weights.shape, 1).astype(jnp.float32)
    own_lane = lax.broadcasted_iota(jnp.int32, (padded, 128), 1)
    own_row = lax.broadcasted_iota(jnp.int32, (padded, 128), 0)
    same_chunk = own_lane >= own_row
    shares = []
    for source in range(kern_count):
        if source == 0:
            block = own_taps[...].astype(jnp.float32)
        else:
            tap_copies[source - 1].wait_recv()
            block = all_taps[source].astype(jnp.float32)
        picked = jnp.where(slot_ids == block[7:8, 112:113], weights, 0.0)
        shares.append(jnp.sum(picked, axis=1, keepdims=True) / total)
        for part in range(2):
            first = (2 * source + part) * padded
            before = jnp.zeros((padded, 128), jnp.float32)
            for chunk in range(chunk_count):
                at = 8 * part + chunk
                row = jnp.broadcast_to(block[at : at + 1], (padded, 128))
                turned = pltpu.roll(row, 0, 1, stride=1, stride_axis=0)
                toeplitz[first : first + padded, chunk * 128 : (chunk + 1) * 128] = jnp.where(
                    same_chunk, turned, before
                ).astype(jnp.bfloat16)
                before = turned

    fields[...] = jnp.dot(toeplitz[...], shifted[...], preferred_element_type=jnp.float32)

    row_at = lax.broadcasted_iota(jnp.int32, (padded, lanes), 0)
    col_at = lax.broadcasted_iota(jnp.int32, (padded, lanes), 1)
    clip_row = tile * rows - margin + row_at
    clip_col = kern * share - margin + col_at
    for block in range(1, BLOCKS):
        later = col_at >= block * reach
        clip_row = jnp.where(later, clip_row + height, clip_row)
        clip_col = jnp.where(later, clip_col - reach, clip_col)
    inside = jnp.logical_and(
        jnp.logical_and(clip_row >= 0, clip_row < clip_rows),
        jnp.logical_and(clip_col >= 0, clip_col < clip_cols),
    )
    inside = jnp.logical_and(inside, row_at < height)
    target = side_by_side(target_rows, TARGET_HALO - margin, padded, margin)
    aerial = jnp.zeros((padded, lanes), jnp.float32)
    for source in range(kern_count):
        first = 2 * source * padded
        real = fields[first : first + padded, :]
        imag = fields[first + padded : first + 2 * padded, :]
        aerial = aerial + shares[source] * (real * real + imag * imag)
    resist = 1.0 / (1.0 + jnp.exp(-SLOPE_FACTOR * (aerial - LEVEL_VALUE)))
    sense = 2.0 * (resist - target) * SLOPE_FACTOR * resist * (1.0 - resist)
    sense = jnp.where(inside, sense, 0.0)
    for source in range(kern_count):
        scaled = (2.0 * shares[source]) * sense
        for part in range(2):
            first = (2 * source + part) * padded
            adjoint[first : first + padded, :] = (
                scaled * fields[first : first + padded, :]
            ).astype(jnp.bfloat16)
    for block in range(BLOCKS):
        piece = pltpu.roll(resist, lanes - block * reach - margin, 1)[:, :share]
        resist_rows[block * height : block * height + padded, :] = piece
    resist_own[...] = resist_rows[margin : margin + rows, :]
    resist_store = pltpu.make_async_copy(resist_own, resist_out, store_sem.at[0])
    resist_store.start()

    spread[...] = lax.dot_general(
        toeplitz[...], adjoint[...], (((0,), (0,)), ((), ())), preferred_element_type=jnp.float32
    )

    gathered = spread[0:PITCH, :]
    for column in range(1, span):
        place = column * PITCH
        gathered = gathered + pltpu.roll(spread[place : place + PITCH, :], column, 1)
    grad_rows[...] = jnp.zeros_like(grad_rows)
    for block in range(BLOCKS):
        piece = pltpu.roll(gathered, lanes - block * reach - 2 * margin, 1)[:, :share]
        grad_rows[block * height : block * height + PITCH, :] += piece
    grad_own[...] = grad_rows[2 * margin : 2 * margin + rows, :]
    grad_store = pltpu.make_async_copy(grad_own, grad_out, store_sem.at[1])
    grad_store.start()

    for copy in tap_copies:
        copy.wait_send()
    pl.when(has_up)(upward.wait_send)
    pl.when(has_down)(downward.wait_send)
    resist_store.wait()
    grad_store.wait()


def hand_over_kernel(grad_in, resist_in, grad_out, resist_out, held, sems):
    images = ((grad_in, grad_out), (resist_in, resist_out))
    loads, stores = [], []
    for at, (taken, given) in enumerate(images):
        loads.append(pltpu.make_async_copy(taken, held.at[at], sems.at[at]))
        stores.append(pltpu.make_async_copy(held.at[at], given, sems.at[2 + at]))
    for load in loads:
        load.start()
    for load, store in zip(loads, stores):
        load.wait()
        store.start()
    for store in stores:
        store.wait()


def on_device(mask, target, kernels, source_weight, assign):
    rows, col_count = mask.shape
    span = kernels.shape[-1]
    margin = (span - 1) // 2
    kern_count = lax.axis_size("kern")
    tile_count = lax.axis_size("tile")
    share = col_count // kern_count
    reach = share + 4 * margin
    width = -(-reach // 128) * 128
    lanes = -(-BLOCKS * reach // 128) * 128
    depth = -(-span * PITCH // 128) * 128
    height = (rows + 2 * margin) // BLOCKS
    padded = -(-height // 16) * 16
    parts = 2 * kern_count
    halo = MASK_HALO + TARGET_HALO
    image = jax.ShapeDtypeStruct((rows, share), jnp.float32)
    images = pl.pallas_call(
        functools.partial(gradient_kernel, (kern_count, tile_count, span, share, width)),
        out_shape=(image, image),
        in_specs=[IN_ANY] * 5,
        out_specs=(IN_ANY, IN_ANY),
        scratch_shapes=[
            pltpu.VMEM((rows, width + 128), jnp.float32),
            pltpu.VMEM((rows, width + 128), jnp.int32),
            pltpu.VMEM((halo, width), jnp.bfloat16),
            pltpu.VMEM((halo, width), jnp.bfloat16),
            pltpu.VMEM((halo, width), jnp.bfloat16),
            pltpu.VMEM((halo, width), jnp.bfloat16),
            pltpu.VMEM((2, 128, 128), jnp.float32),
            pltpu.VMEM((16, 128), jnp.float32),
            pltpu.VMEM((16, 128), jnp.bfloat16),
            pltpu.VMEM((kern_count, 16, 128), jnp.bfloat16),
            pltpu.VMEM((rows + 2 * MASK_HALO, width), jnp.float32),
            pltpu.VMEM((rows + 2 * TARGET_HALO, width), jnp.float32),
            pltpu.VMEM((parts * padded, depth), jnp.bfloat16),
            pltpu.VMEM((depth, lanes), jnp.bfloat16),
            pltpu.VMEM((parts * padded, lanes), jnp.float32),
            pltpu.VMEM((parts * padded, lanes), jnp.bfloat16),
            pltpu.VMEM((depth, lanes), jnp.float32),
            pltpu.VMEM(((BLOCKS - 1) * height + padded, share), jnp.float32),
            pltpu.VMEM(((BLOCKS - 1) * height + PITCH, share), jnp.float32),
            pltpu.VMEM((rows, share), jnp.float32),
            pltpu.VMEM((rows, share), jnp.float32),
            pltpu.VMEM(kernels.shape[2:3] + kernels.shape[1:2] + kernels.shape[3:], kernels.dtype),
            pltpu.VMEM((1, source_weight.shape[0]), jnp.float32),
            pltpu.SMEM((1,), jnp.int32),
            pltpu.SemaphoreType.DMA((5,)),
            pltpu.SemaphoreType.DMA((2,)),
            pltpu.SemaphoreType.DMA((kern_count,)),
            pltpu.SemaphoreType.DMA((kern_count,)),
            pltpu.SemaphoreType.DMA((2,)),
            pltpu.SemaphoreType.DMA((2,)),
        ],
        compiler_params=pltpu.CompilerParams(
            collective_id=0, has_side_effects=True, vmem_limit_bytes=56 * 1024 * 1024
        ),
        name="image_gradient",
    )(mask, target, jnp.swapaxes(kernels[0], 0, 1), source_weight[None, :], assign)
    return pl.pallas_call(
        hand_over_kernel,
        out_shape=(image, image),
        in_specs=[IN_ANY, IN_ANY],
        out_specs=(IN_ANY, IN_ANY),
        scratch_shapes=[
            pltpu.VMEM((2, rows, share), jnp.float32),
            pltpu.SemaphoreType.DMA((4,)),
        ],
        compiler_params=pltpu.CompilerParams(vmem_limit_bytes=56 * 1024 * 1024),
        name="hand_over",
    )(*images)


def solution(mesh):
    placed = (P("tile", None), P("tile", None), P("kern", None, None, None), P(), P("kern"))
    return jax.shard_map(
        on_device,
        mesh=mesh,
        in_specs=placed,
        out_specs=(P("tile", "kern"), P("tile", "kern")),
        check_vma=False,
    )
```

```python
import functools

import jax
import jax.numpy as jnp
from jax import lax
from jax.experimental import pallas as pl
from jax.experimental.pallas import tpu as pltpu
from jax.sharding import PartitionSpec as P

SLOPE_FACTOR = 4.0
LEVEL_VALUE = 0.6
BLOCKS = 3
PITCH = 48
MASK_HALO = 32
TARGET_HALO = 16
MESH = pl.DeviceIdType.MESH
IN_VMEM = pl.BlockSpec(memory_space=pltpu.VMEM)
IN_ANY = pl.BlockSpec(memory_space=pl.ANY)


def gradient_kernel(
    sizes, mask_hbm, target_hbm, kernel_hbm, weight_hbm, assign_hbm, grad_out, resist_out,
    mask_window, target_window, send_up, send_down, above, below, square, tap_rows, own_taps,
    all_taps, mask_rows, target_rows, toeplitz, shifted, fields, adjoint, spread, resist_rows,
    grad_rows, kernel_ref, weight_ref, assign_own, load_sem, tap_send, tap_recv, halo_send, halo_recv,
):
    kern_count, tile_count, span, share, width = sizes
    tile = lax.axis_index("tile")
    kern = lax.axis_index("kern")
    rows, clip_cols = mask_hbm.shape
    clip_rows = rows * tile_count
    margin = (span - 1) // 2
    height = (rows + 2 * margin) // BLOCKS
    padded = -(-height // 16) * 16
    depth = toeplitz.shape[1]
    reach = share + 4 * margin
    lanes = shifted.shape[1]
    has_up = tile > 0
    has_down = tile < tile_count - 1

    barrier = pltpu.get_barrier_semaphore()
    for step in range(1, kern_count):
        peer = lax.rem(kern + step, kern_count)
        pl.semaphore_signal(barrier, inc=1, device_id=(tile, peer), device_id_type=MESH)

    @pl.when(has_up)
    def _():
        pl.semaphore_signal(barrier, inc=1, device_id=(tile - 1, kern), device_id_type=MESH)

    @pl.when(has_down)
    def _():
        pl.semaphore_signal(barrier, inc=1, device_id=(tile + 1, kern), device_id_type=MESH)

    start = kern * share - 2 * margin
    loaded = width + 128
    base = (start + 128) // 128 * 128 - 128
    base = jnp.minimum(jnp.maximum(base, 0), clip_cols - loaded)
    base = pl.multiple_of(base, 128)
    small_loads = [
        pltpu.make_async_copy(kernel_hbm, kernel_ref, load_sem.at[2]),
        pltpu.make_async_copy(weight_hbm, weight_ref, load_sem.at[3]),
        pltpu.make_async_copy(assign_hbm, assign_own, load_sem.at[4]),
    ]
    for load in small_loads:
        load.start()
    loads = [
        pltpu.make_async_copy(mask_hbm.at[:, pl.ds(base, loaded)], mask_window, load_sem.at[0]),
        pltpu.make_async_copy(target_hbm.at[:, pl.ds(base, loaded)], target_window, load_sem.at[1]),
    ]
    for load in loads:
        load.start()

    square[...] = jnp.zeros_like(square)
    for load in small_loads:
        load.wait()
    for row in range(span):
        pair = kernel_ref[row].astype(jnp.float32)
        square[0, row : row + 1, 0:span] = pair[0:1]
        square[1, row : row + 1, 0:span] = pair[1:2]
    lane = lax.broadcasted_iota(jnp.int32, (1, 128), 1)
    chunk_count = depth // 128
    for part in range(2):
        turned = square[part].T
        chunks = [jnp.zeros((1, 128), jnp.float32)] * chunk_count
        for column in range(span):
            chunk, offset = divmod(column * PITCH, 128)
            row = turned[column : column + 1]
            row = pltpu.roll(row, offset, 1) if offset else row
            if offset + span <= 128:
                chunks[chunk] = chunks[chunk] + row
            else:
                chunks[chunk] = chunks[chunk] + jnp.where(lane >= offset, row, 0.0)
                chunks[chunk + 1] = chunks[chunk + 1] + jnp.where(lane < offset, row, 0.0)
        mark = assign_own[0].astype(jnp.float32)
        chunks[-1] = jnp.where(lane >= 112, mark, chunks[-1])
        for chunk in range(chunk_count):
            tap_rows[8 * part + chunk : 8 * part + chunk + 1, :] = chunks[chunk]
    own_taps[...] = tap_rows[...].astype(jnp.bfloat16)

    for load in loads:
        load.wait()
    clip_col = start + lax.broadcasted_iota(jnp.int32, (rows, width), 1)
    col_inside = jnp.logical_and(clip_col >= 0, clip_col < clip_cols)
    back = lax.rem(base - start + loaded, loaded)
    mask_own = pltpu.roll(mask_window[...], back, 1)[:, :width]
    mask_own = jnp.where(col_inside, mask_own, 0.0).astype(jnp.bfloat16)
    target_own = pltpu.roll(target_window[...].astype(jnp.float32), back, 1)[:, :width]
    target_own = target_own.astype(jnp.bfloat16)
    send_up[0:MASK_HALO, :] = mask_own[0:MASK_HALO]
    send_up[MASK_HALO:, :] = target_own[0:TARGET_HALO]
    send_down[0:MASK_HALO, :] = mask_own[rows - MASK_HALO :]
    send_down[MASK_HALO:, :] = target_own[rows - TARGET_HALO :]
    upward = pltpu.make_async_remote_copy(
        src_ref=send_up,
        dst_ref=below,
        send_sem=halo_send.at[0],
        recv_sem=halo_recv.at[0],
        device_id=(tile - 1, kern),
        device_id_type=MESH,
    )
    downward = pltpu.make_async_remote_copy(
        src_ref=send_down,
        dst_ref=above,
        send_sem=halo_send.at[1],
        recv_sem=halo_recv.at[1],
        device_id=(tile + 1, kern),
        device_id_type=MESH,
    )
    pl.semaphore_wait(barrier, kern_count - 1 + has_up.astype(jnp.int32) + has_down.astype(jnp.int32))
    tap_copies = []
    for step in range(1, kern_count):
        peer = lax.rem(kern + step, kern_count)
        tap_copies.append(
            pltpu.make_async_remote_copy(
                src_ref=own_taps,
                dst_ref=all_taps.at[step],
                send_sem=tap_send.at[step],
                recv_sem=tap_recv.at[step],
                device_id=(tile, peer),
                device_id_type=MESH,
            )
        )
    for copy in tap_copies:
        copy.start()
    pl.when(has_up)(upward.start)
    pl.when(has_down)(downward.start)
    mask_rows[MASK_HALO : MASK_HALO + rows, :] = mask_own.astype(jnp.float32)
    target_rows[TARGET_HALO : TARGET_HALO + rows, :] = target_own.astype(jnp.float32)

    @pl.when(has_up)
    def _():
        downward.wait_recv()

    @pl.when(jnp.logical_not(has_up))
    def _():
        above[...] = jnp.zeros_like(above)

    @pl.when(has_down)
    def _():
        upward.wait_recv()

    @pl.when(jnp.logical_not(has_down))
    def _():
        below[...] = jnp.zeros_like(below)

    mask_rows[0:MASK_HALO, :] = above[0:MASK_HALO, :].astype(jnp.float32)
    mask_rows[MASK_HALO + rows :, :] = below[0:MASK_HALO, :].astype(jnp.float32)
    target_rows[0:TARGET_HALO, :] = above[MASK_HALO:, :].astype(jnp.float32)
    target_rows[TARGET_HALO + rows :, :] = below[MASK_HALO:, :].astype(jnp.float32)

    def side_by_side(held, top, count, shift):
        pieces = []
        for block in range(BLOCKS):
            piece = held[top + block * height : top + block * height + count, :]
            piece = pltpu.roll(piece, width - shift, 1) if shift else piece
            pieces.append(piece[:, :reach])
        if lanes > BLOCKS * reach:
            pieces.append(jnp.zeros((count, lanes - BLOCKS * reach), jnp.float32))
        return jnp.concatenate(pieces, axis=1)

    window = side_by_side(mask_rows, MASK_HALO - 2 * margin, PITCH, 0)
    for column in range(span):
        turned = window if column == 0 else pltpu.roll(window, lanes - column, 1)
        shifted[column * PITCH : (column + 1) * PITCH, :] = turned.astype(jnp.bfloat16)
    shifted[span * PITCH :, :] = jnp.zeros((depth - span * PITCH, lanes), jnp.bfloat16)

    weights = weight_ref[...]
    total = jnp.sum(weights, axis=1, keepdims=True)
    slot_ids = lax.broadcasted_iota(jnp.int32, weights.shape, 1).astype(jnp.float32)
    own_lane = lax.broadcasted_iota(jnp.int32, (padded, 128), 1)
    own_row = lax.broadcasted_iota(jnp.int32, (padded, 128), 0)
    same_chunk = own_lane >= own_row
    shares = []
    for source in range(kern_count):
        if source == 0:
            block = own_taps[...].astype(jnp.float32)
        else:
            tap_copies[source - 1].wait_recv()
            block = all_taps[source].astype(jnp.float32)
        picked = jnp.where(slot_ids == block[7:8, 112:113], weights, 0.0)
        shares.append(jnp.sum(picked, axis=1, keepdims=True) / total)
        for part in range(2):
            first = (2 * source + part) * padded
            before = jnp.zeros((padded, 128), jnp.float32)
            for chunk in range(chunk_count):
                at = 8 * part + chunk
                row = jnp.broadcast_to(block[at : at + 1], (padded, 128))
                turned = pltpu.roll(row, 0, 1, stride=1, stride_axis=0)
                toeplitz[first : first + padded, chunk * 128 : (chunk + 1) * 128] = jnp.where(
                    same_chunk, turned, before
                ).astype(jnp.bfloat16)
                before = turned

    fields[...] = jnp.dot(toeplitz[...], shifted[...], preferred_element_type=jnp.float32)

    row_at = lax.broadcasted_iota(jnp.int32, (padded, lanes), 0)
    col_at = lax.broadcasted_iota(jnp.int32, (padded, lanes), 1)
    clip_row = tile * rows - margin + row_at
    clip_col = kern * share - margin + col_at
    for block in range(1, BLOCKS):
        later = col_at >= block * reach
        clip_row = jnp.where(later, clip_row + height, clip_row)
        clip_col = jnp.where(later, clip_col - reach, clip_col)
    inside = jnp.logical_and(
        jnp.logical_and(clip_row >= 0, clip_row < clip_rows),
        jnp.logical_and(clip_col >= 0, clip_col < clip_cols),
    )
    inside = jnp.logical_and(inside, row_at < height)
    target = side_by_side(target_rows, TARGET_HALO - margin, padded, margin)
    aerial = jnp.zeros((padded, lanes), jnp.float32)
    for source in range(kern_count):
        first = 2 * source * padded
        real = fields[first : first + padded, :]
        imag = fields[first + padded : first + 2 * padded, :]
        aerial = aerial + shares[source] * (real * real + imag * imag)
    resist = 1.0 / (1.0 + jnp.exp(-SLOPE_FACTOR * (aerial - LEVEL_VALUE)))
    sense = 2.0 * (resist - target) * SLOPE_FACTOR * resist * (1.0 - resist)
    sense = jnp.where(inside, sense, 0.0)
    for source in range(kern_count):
        scaled = (2.0 * shares[source]) * sense
        for part in range(2):
            first = (2 * source + part) * padded
            adjoint[first : first + padded, :] = (
                scaled * fields[first : first + padded, :]
            ).astype(jnp.bfloat16)
    for block in range(BLOCKS):
        piece = pltpu.roll(resist, lanes - block * reach - margin, 1)[:, :share]
        resist_rows[block * height : block * height + padded, :] = piece
    resist_out[...] = resist_rows[margin : margin + rows, :]

    spread[...] = lax.dot_general(
        toeplitz[...], adjoint[...], (((0,), (0,)), ((), ())), preferred_element_type=jnp.float32
    )

    gathered = spread[0:PITCH, :]
    for column in range(1, span):
        place = column * PITCH
        gathered = gathered + pltpu.roll(spread[place : place + PITCH, :], column, 1)
    grad_rows[...] = jnp.zeros_like(grad_rows)
    for block in range(BLOCKS):
        piece = pltpu.roll(gathered, lanes - block * reach - 2 * margin, 1)[:, :share]
        grad_rows[block * height : block * height + PITCH, :] += piece
    grad_out[...] = grad_rows[2 * margin : 2 * margin + rows, :]

    for copy in tap_copies:
        copy.wait_send()
    pl.when(has_up)(upward.wait_send)
    pl.when(has_down)(downward.wait_send)


def hand_over_kernel(grad_in, resist_in, grad_out, resist_out, sems):
    moves = [
        pltpu.make_async_copy(grad_in, grad_out, sems.at[0]),
        pltpu.make_async_copy(resist_in, resist_out, sems.at[1]),
    ]
    for move in moves:
        move.start()
    for move in moves:
        move.wait()


def on_device(mask, target, kernels, source_weight, assign):
    rows, col_count = mask.shape
    span = kernels.shape[-1]
    margin = (span - 1) // 2
    kern_count = lax.axis_size("kern")
    tile_count = lax.axis_size("tile")
    share = col_count // kern_count
    reach = share + 4 * margin
    width = -(-reach // 128) * 128
    lanes = -(-BLOCKS * reach // 128) * 128
    depth = -(-span * PITCH // 128) * 128
    height = (rows + 2 * margin) // BLOCKS
    padded = -(-height // 16) * 16
    parts = 2 * kern_count
    halo = MASK_HALO + TARGET_HALO
    image = jax.ShapeDtypeStruct((rows, share), jnp.float32)
    images = pl.pallas_call(
        functools.partial(gradient_kernel, (kern_count, tile_count, span, share, width)),
        out_shape=(image, image),
        in_specs=[IN_ANY] * 5,
        out_specs=(IN_VMEM, IN_VMEM),
        scratch_shapes=[
            pltpu.VMEM((rows, width + 128), jnp.float32),
            pltpu.VMEM((rows, width + 128), jnp.int32),
            pltpu.VMEM((halo, width), jnp.bfloat16),
            pltpu.VMEM((halo, width), jnp.bfloat16),
            pltpu.VMEM((halo, width), jnp.bfloat16),
            pltpu.VMEM((halo, width), jnp.bfloat16),
            pltpu.VMEM((2, 128, 128), jnp.float32),
            pltpu.VMEM((16, 128), jnp.float32),
            pltpu.VMEM((16, 128), jnp.bfloat16),
            pltpu.VMEM((kern_count, 16, 128), jnp.bfloat16),
            pltpu.VMEM((rows + 2 * MASK_HALO, width), jnp.float32),
            pltpu.VMEM((rows + 2 * TARGET_HALO, width), jnp.float32),
            pltpu.VMEM((parts * padded, depth), jnp.bfloat16),
            pltpu.VMEM((depth, lanes), jnp.bfloat16),
            pltpu.VMEM((parts * padded, lanes), jnp.float32),
            pltpu.VMEM((parts * padded, lanes), jnp.bfloat16),
            pltpu.VMEM((depth, lanes), jnp.float32),
            pltpu.VMEM(((BLOCKS - 1) * height + padded, share), jnp.float32),
            pltpu.VMEM(((BLOCKS - 1) * height + PITCH, share), jnp.float32),
            pltpu.VMEM(kernels.shape[2:3] + kernels.shape[1:2] + kernels.shape[3:], kernels.dtype),
            pltpu.VMEM((1, source_weight.shape[0]), jnp.float32),
            pltpu.SMEM((1,), jnp.int32),
            pltpu.SemaphoreType.DMA((5,)),
            pltpu.SemaphoreType.DMA((kern_count,)),
            pltpu.SemaphoreType.DMA((kern_count,)),
            pltpu.SemaphoreType.DMA((2,)),
            pltpu.SemaphoreType.DMA((2,)),
        ],
        compiler_params=pltpu.CompilerParams(
            collective_id=0, has_side_effects=True, vmem_limit_bytes=55040 * 1024
        ),
        name="image_gradient",
    )(mask, target, jnp.swapaxes(kernels[0], 0, 1), source_weight[None, :], assign)
    return pl.pallas_call(
        hand_over_kernel,
        out_shape=(image, image),
        in_specs=[IN_VMEM, IN_VMEM],
        out_specs=(IN_ANY, IN_ANY),
        scratch_shapes=[pltpu.SemaphoreType.DMA((2,))],
        compiler_params=pltpu.CompilerParams(vmem_limit_bytes=1024 * 1024),
        name="hand_over",
    )(*images)


def solution(mesh):
    placed = (P("tile", None), P("tile", None), P("kern", None, None, None), P(), P("kern"))
    return jax.shard_map(
        on_device,
        mesh=mesh,
        in_specs=placed,
        out_specs=(P("tile", "kern"), P("tile", "kern")),
        check_vma=False,
    )
```

```python
import functools

import jax
import jax.numpy as jnp
from jax import lax
from jax.experimental import pallas as pl
from jax.experimental.pallas import tpu as pltpu
from jax.sharding import PartitionSpec as P

SLOPE_FACTOR = 4.0
LEVEL_VALUE = 0.6
BLOCKS = 3
PITCH = 48
MASK_HALO = 32
TARGET_HALO = 16
MESH = pl.DeviceIdType.MESH
IN_VMEM = pl.BlockSpec(memory_space=pltpu.VMEM)
IN_ANY = pl.BlockSpec(memory_space=pl.ANY)


def window_of(mask_hbm, target_hbm, mask_window, target_window, sems, share, margin):
    rows, clip_cols = mask_hbm.shape
    loaded = mask_window.shape[1]
    width = loaded - 128
    start = lax.axis_index("kern") * share - 2 * margin
    base = (start + 128) // 128 * 128 - 128
    base = jnp.minimum(jnp.maximum(base, 0), clip_cols - loaded)
    base = pl.multiple_of(base, 128)
    loads = [
        pltpu.make_async_copy(mask_hbm.at[:, pl.ds(base, loaded)], mask_window, sems.at[0]),
        pltpu.make_async_copy(target_hbm.at[:, pl.ds(base, loaded)], target_window, sems.at[1]),
    ]

    def finish():
        for load in loads:
            load.wait()
        clip_col = start + lax.broadcasted_iota(jnp.int32, (rows, width), 1)
        col_inside = jnp.logical_and(clip_col >= 0, clip_col < clip_cols)
        back = lax.rem(base - start + loaded, loaded)
        mask_own = pltpu.roll(mask_window[...], back, 1)[:, :width]
        mask_own = jnp.where(col_inside, mask_own, 0.0).astype(jnp.bfloat16)
        target_own = pltpu.roll(target_window[...].astype(jnp.float32), back, 1)[:, :width]
        return mask_own, target_own.astype(jnp.bfloat16)

    return loads, finish


def exchange_kernel(
    sizes, mask_hbm, target_hbm, kernel_hbm, assign_hbm, all_taps, above, below,
    mask_window, target_window, send_up, send_down, square, tap_rows, own_taps, kernel_ref,
    assign_own, load_sem, own_sem, tap_send, tap_recv, halo_send, halo_recv,
):
    kern_count, tile_count, span, share = sizes
    tile = lax.axis_index("tile")
    kern = lax.axis_index("kern")
    rows = mask_hbm.shape[0]
    margin = (span - 1) // 2
    depth = -(-span * PITCH // 128) * 128
    has_up = tile > 0
    has_down = tile < tile_count - 1

    barrier = pltpu.get_barrier_semaphore()
    for step in range(1, kern_count):
        peer = lax.rem(kern + step, kern_count)
        pl.semaphore_signal(barrier, inc=1, device_id=(tile, peer), device_id_type=MESH)

    @pl.when(has_up)
    def _():
        pl.semaphore_signal(barrier, inc=1, device_id=(tile - 1, kern), device_id_type=MESH)

    @pl.when(has_down)
    def _():
        pl.semaphore_signal(barrier, inc=1, device_id=(tile + 1, kern), device_id_type=MESH)

    small_loads = [
        pltpu.make_async_copy(kernel_hbm, kernel_ref, load_sem.at[2]),
        pltpu.make_async_copy(assign_hbm, assign_own, load_sem.at[3]),
    ]
    loads, finish = window_of(
        mask_hbm, target_hbm, mask_window, target_window, load_sem, share, margin
    )
    for load in small_loads + loads:
        load.start()

    square[...] = jnp.zeros_like(square)
    for load in small_loads:
        load.wait()
    for row in range(span):
        pair = kernel_ref[row].astype(jnp.float32)
        square[0, row : row + 1, 0:span] = pair[0:1]
        square[1, row : row + 1, 0:span] = pair[1:2]
    lane = lax.broadcasted_iota(jnp.int32, (1, 128), 1)
    chunk_count = depth // 128
    for part in range(2):
        turned = square[part].T
        chunks = [jnp.zeros((1, 128), jnp.float32)] * chunk_count
        for column in range(span):
            chunk, offset = divmod(column * PITCH, 128)
            row = turned[column : column + 1]
            row = pltpu.roll(row, offset, 1) if offset else row
            if offset + span <= 128:
                chunks[chunk] = chunks[chunk] + row
            else:
                chunks[chunk] = chunks[chunk] + jnp.where(lane >= offset, row, 0.0)
                chunks[chunk + 1] = chunks[chunk + 1] + jnp.where(lane < offset, row, 0.0)
        mark = assign_own[0].astype(jnp.float32)
        chunks[-1] = jnp.where(lane >= 112, mark, chunks[-1])
        for chunk in range(chunk_count):
            tap_rows[8 * part + chunk : 8 * part + chunk + 1, :] = chunks[chunk]
    own_taps[...] = tap_rows[...].astype(jnp.bfloat16)

    own_copy = pltpu.make_async_copy(own_taps, all_taps.at[0], own_sem)
    own_copy.start()
    mask_own, target_own = finish()
    send_up[0:MASK_HALO, :] = mask_own[0:MASK_HALO]
    send_up[MASK_HALO:, :] = target_own[0:TARGET_HALO]
    send_down[0:MASK_HALO, :] = mask_own[rows - MASK_HALO :]
    send_down[MASK_HALO:, :] = target_own[rows - TARGET_HALO :]
    upward = pltpu.make_async_remote_copy(
        src_ref=send_up,
        dst_ref=below,
        send_sem=halo_send.at[0],
        recv_sem=halo_recv.at[0],
        device_id=(tile - 1, kern),
        device_id_type=MESH,
    )
    downward = pltpu.make_async_remote_copy(
        src_ref=send_down,
        dst_ref=above,
        send_sem=halo_send.at[1],
        recv_sem=halo_recv.at[1],
        device_id=(tile + 1, kern),
        device_id_type=MESH,
    )
    pl.semaphore_wait(barrier, kern_count - 1 + has_up.astype(jnp.int32) + has_down.astype(jnp.int32))
    tap_copies = []
    for step in range(1, kern_count):
        peer = lax.rem(kern + step, kern_count)
        tap_copies.append(
            pltpu.make_async_remote_copy(
                src_ref=own_taps,
                dst_ref=all_taps.at[step],
                send_sem=tap_send.at[step],
                recv_sem=tap_recv.at[step],
                device_id=(tile, peer),
                device_id_type=MESH,
            )
        )
    for copy in tap_copies:
        copy.start()
    pl.when(has_up)(upward.start)
    pl.when(has_down)(downward.start)
    own_copy.wait()
    for copy in tap_copies:
        copy.wait()
    pl.when(has_up)(upward.wait_send)
    pl.when(has_down)(downward.wait_send)
    pl.when(has_up)(downward.wait_recv)
    pl.when(has_down)(upward.wait_recv)


def gradient_kernel(
    sizes, mask_hbm, target_hbm, weight_hbm, taps_hbm, above_hbm, below_hbm, grad_out, resist_out,
    mask_window, target_window, weight_ref, all_taps, above, below, mask_rows, target_rows, toeplitz,
    shifted, fields, adjoint, spread, resist_rows, grad_rows, resist_own, grad_own, load_sem, store_sem,
):
    kern_count, tile_count, span, share = sizes
    tile = lax.axis_index("tile")
    kern = lax.axis_index("kern")
    rows, clip_cols = mask_hbm.shape
    clip_rows = rows * tile_count
    margin = (span - 1) // 2
    height = (rows + 2 * margin) // BLOCKS
    padded = -(-height // 16) * 16
    depth = toeplitz.shape[1]
    chunk_count = depth // 128
    reach = share + 4 * margin
    width = above.shape[1]
    lanes = shifted.shape[1]

    loads, finish = window_of(
        mask_hbm, target_hbm, mask_window, target_window, load_sem, share, margin
    )
    halo_loads = [
        pltpu.make_async_copy(above_hbm, above, load_sem.at[2]),
        pltpu.make_async_copy(below_hbm, below, load_sem.at[3]),
    ]
    tap_loads = [
        pltpu.make_async_copy(taps_hbm, all_taps, load_sem.at[4]),
        pltpu.make_async_copy(weight_hbm, weight_ref, load_sem.at[5]),
    ]
    for load in loads + halo_loads + tap_loads:
        load.start()

    mask_own, target_own = finish()
    mask_rows[MASK_HALO : MASK_HALO + rows, :] = mask_own.astype(jnp.float32)
    target_rows[TARGET_HALO : TARGET_HALO + rows, :] = target_own.astype(jnp.float32)
    for load in halo_loads:
        load.wait()
    for halo, inside, mask_at, target_at in (
        (above, tile > 0, 0, 0),
        (below, tile < tile_count - 1, MASK_HALO + rows, TARGET_HALO + rows),
    ):
        held = jnp.where(inside, halo[...].astype(jnp.float32), 0.0)
        mask_rows[mask_at : mask_at + MASK_HALO, :] = held[0:MASK_HALO]
        target_rows[target_at : target_at + TARGET_HALO, :] = held[MASK_HALO:]

    def side_by_side(held, top, count, shift):
        pieces = []
        for block in range(BLOCKS):
            piece = held[top + block * height : top + block * height + count, :]
            piece = pltpu.roll(piece, width - shift, 1) if shift else piece
            pieces.append(piece[:, :reach])
        if lanes > BLOCKS * reach:
            pieces.append(jnp.zeros((count, lanes - BLOCKS * reach), jnp.float32))
        return jnp.concatenate(pieces, axis=1)

    window = side_by_side(mask_rows, MASK_HALO - 2 * margin, PITCH, 0)
    for column in range(span):
        turned = window if column == 0 else pltpu.roll(window, lanes - column, 1)
        shifted[column * PITCH : (column + 1) * PITCH, :] = turned.astype(jnp.bfloat16)
    shifted[span * PITCH :, :] = jnp.zeros((depth - span * PITCH, lanes), jnp.bfloat16)

    for load in tap_loads:
        load.wait()
    weights = weight_ref[...]
    total = jnp.sum(weights, axis=1, keepdims=True)
    slot_ids = lax.broadcasted_iota(jnp.int32, weights.shape, 1).astype(jnp.float32)
    own_lane = lax.broadcasted_iota(jnp.int32, (padded, 128), 1)
    own_row = lax.broadcasted_iota(jnp.int32, (padded, 128), 0)
    same_chunk = own_lane >= own_row
    shares = []
    for source in range(kern_count):
        block = all_taps[source].astype(jnp.float32)
        picked = jnp.where(slot_ids == block[7:8, 112:113], weights, 0.0)
        shares.append(jnp.sum(picked, axis=1, keepdims=True) / total)
        for part in range(2):
            first = (2 * source + part) * padded
            before = jnp.zeros((padded, 128), jnp.float32)
            for chunk in range(chunk_count):
                at = 8 * part + chunk
                row = jnp.broadcast_to(block[at : at + 1], (padded, 128))
                turned = pltpu.roll(row, 0, 1, stride=1, stride_axis=0)
                toeplitz[first : first + padded, chunk * 128 : (chunk + 1) * 128] = jnp.where(
                    same_chunk, turned, before
                ).astype(jnp.bfloat16)
                before = turned

    fields[...] = jnp.dot(toeplitz[...], shifted[...], preferred_element_type=jnp.float32)

    row_at = lax.broadcasted_iota(jnp.int32, (padded, lanes), 0)
    col_at = lax.broadcasted_iota(jnp.int32, (padded, lanes), 1)
    clip_row = tile * rows - margin + row_at
    clip_col = kern * share - margin + col_at
    for block in range(1, BLOCKS):
        later = col_at >= block * reach
        clip_row = jnp.where(later, clip_row + height, clip_row)
        clip_col = jnp.where(later, clip_col - reach, clip_col)
    inside = jnp.logical_and(
        jnp.logical_and(clip_row >= 0, clip_row < clip_rows),
        jnp.logical_and(clip_col >= 0, clip_col < clip_cols),
    )
    inside = jnp.logical_and(inside, row_at < height)
    target = side_by_side(target_rows, TARGET_HALO - margin, padded, margin)
    aerial = jnp.zeros((padded, lanes), jnp.float32)
    for source in range(kern_count):
        first = 2 * source * padded
        real = fields[first : first + padded, :]
        imag = fields[first + padded : first + 2 * padded, :]
        aerial = aerial + shares[source] * (real * real + imag * imag)
    resist = 1.0 / (1.0 + jnp.exp(-SLOPE_FACTOR * (aerial - LEVEL_VALUE)))
    sense = 2.0 * (resist - target) * SLOPE_FACTOR * resist * (1.0 - resist)
    sense = jnp.where(inside, sense, 0.0)
    for source in range(kern_count):
        scaled = (2.0 * shares[source]) * sense
        for part in range(2):
            first = (2 * source + part) * padded
            adjoint[first : first + padded, :] = (
                scaled * fields[first : first + padded, :]
            ).astype(jnp.bfloat16)
    for block in range(BLOCKS):
        piece = pltpu.roll(resist, lanes - block * reach - margin, 1)[:, :share]
        resist_rows[block * height : block * height + padded, :] = piece
    resist_own[...] = resist_rows[margin : margin + rows, :]
    resist_store = pltpu.make_async_copy(resist_own, resist_out, store_sem.at[0])
    resist_store.start()

    spread[...] = lax.dot_general(
        toeplitz[...], adjoint[...], (((0,), (0,)), ((), ())), preferred_element_type=jnp.float32
    )

    gathered = spread[0:PITCH, :]
    for column in range(1, span):
        place = column * PITCH
        gathered = gathered + pltpu.roll(spread[place : place + PITCH, :], column, 1)
    grad_rows[...] = jnp.zeros_like(grad_rows)
    for block in range(BLOCKS):
        piece = pltpu.roll(gathered, lanes - block * reach - 2 * margin, 1)[:, :share]
        grad_rows[block * height : block * height + PITCH, :] += piece
    grad_own[...] = grad_rows[2 * margin : 2 * margin + rows, :]
    grad_store = pltpu.make_async_copy(grad_own, grad_out, store_sem.at[1])
    grad_store.start()

    resist_store.wait()
    grad_store.wait()


def on_device(mask, target, kernels, source_weight, assign):
    rows, col_count = mask.shape
    span = kernels.shape[-1]
    margin = (span - 1) // 2
    kern_count = lax.axis_size("kern")
    tile_count = lax.axis_size("tile")
    share = col_count // kern_count
    reach = share + 4 * margin
    width = -(-reach // 128) * 128
    lanes = -(-BLOCKS * reach // 128) * 128
    depth = -(-span * PITCH // 128) * 128
    height = (rows + 2 * margin) // BLOCKS
    padded = -(-height // 16) * 16
    parts = 2 * kern_count
    halo = MASK_HALO + TARGET_HALO
    sizes = (kern_count, tile_count, span, share)
    limit = 56 * 1024 * 1024
    by_row = jnp.swapaxes(kernels[0], 0, 1)
    taps, above, below = pl.pallas_call(
        functools.partial(exchange_kernel, sizes),
        out_shape=(
            jax.ShapeDtypeStruct((kern_count, 16, 128), jnp.bfloat16),
            jax.ShapeDtypeStruct((halo, width), jnp.bfloat16),
            jax.ShapeDtypeStruct((halo, width), jnp.bfloat16),
        ),
        in_specs=[IN_ANY] * 4,
        out_specs=(IN_ANY,) * 3,
        scratch_shapes=[
            pltpu.VMEM((rows, width + 128), jnp.float32),
            pltpu.VMEM((rows, width + 128), jnp.int32),
            pltpu.VMEM((halo, width), jnp.bfloat16),
            pltpu.VMEM((halo, width), jnp.bfloat16),
            pltpu.VMEM((2, 128, 128), jnp.float32),
            pltpu.VMEM((16, 128), jnp.float32),
            pltpu.VMEM((16, 128), jnp.bfloat16),
            pltpu.VMEM(by_row.shape, by_row.dtype),
            pltpu.SMEM((1,), jnp.int32),
            pltpu.SemaphoreType.DMA((4,)),
            pltpu.SemaphoreType.DMA,
            pltpu.SemaphoreType.DMA((kern_count,)),
            pltpu.SemaphoreType.DMA((kern_count,)),
            pltpu.SemaphoreType.DMA((2,)),
            pltpu.SemaphoreType.DMA((2,)),
        ],
        compiler_params=pltpu.CompilerParams(
            collective_id=0, has_side_effects=True, vmem_limit_bytes=limit
        ),
        name="exchange",
    )(mask, target, by_row, assign)
    image = jax.ShapeDtypeStruct((rows, share), jnp.float32)
    return pl.pallas_call(
        functools.partial(gradient_kernel, sizes),
        out_shape=(image, image),
        in_specs=[IN_ANY] * 6,
        out_specs=(IN_ANY, IN_ANY),
        scratch_shapes=[
            pltpu.VMEM((rows, width + 128), jnp.float32),
            pltpu.VMEM((rows, width + 128), jnp.int32),
            pltpu.VMEM((1, source_weight.shape[0]), jnp.float32),
            pltpu.VMEM((kern_count, 16, 128), jnp.bfloat16),
            pltpu.VMEM((halo, width), jnp.bfloat16),
            pltpu.VMEM((halo, width), jnp.bfloat16),
            pltpu.VMEM((rows + 2 * MASK_HALO, width), jnp.float32),
            pltpu.VMEM((rows + 2 * TARGET_HALO, width), jnp.float32),
            pltpu.VMEM((parts * padded, depth), jnp.bfloat16),
            pltpu.VMEM((depth, lanes), jnp.bfloat16),
            pltpu.VMEM((parts * padded, lanes), jnp.float32),
            pltpu.VMEM((parts * padded, lanes), jnp.bfloat16),
            pltpu.VMEM((depth, lanes), jnp.float32),
            pltpu.VMEM(((BLOCKS - 1) * height + padded, share), jnp.float32),
            pltpu.VMEM(((BLOCKS - 1) * height + PITCH, share), jnp.float32),
            pltpu.VMEM((rows, share), jnp.float32),
            pltpu.VMEM((rows, share), jnp.float32),
            pltpu.SemaphoreType.DMA((6,)),
            pltpu.SemaphoreType.DMA((2,)),
        ],
        compiler_params=pltpu.CompilerParams(vmem_limit_bytes=limit),
        name="image_gradient",
    )(mask, target, source_weight[None, :], taps, above, below)


def solution(mesh):
    placed = (P("tile", None), P("tile", None), P("kern", None, None, None), P(), P("kern"))
    return jax.shard_map(
        on_device,
        mesh=mesh,
        in_specs=placed,
        out_specs=(P("tile", "kern"), P("tile", "kern")),
        check_vma=False,
    )
```

```python
import functools

import jax
import jax.numpy as jnp
from jax import lax
from jax.experimental import pallas as pl
from jax.experimental.pallas import tpu as pltpu
from jax.sharding import PartitionSpec as P

SLOPE_FACTOR = 4.0
LEVEL_VALUE = 0.6
BLOCKS = 3
PITCH = 48
MASK_HALO = 32
TARGET_HALO = 16
MESH = pl.DeviceIdType.MESH
IN_VMEM = pl.BlockSpec(memory_space=pltpu.VMEM)
IN_ANY = pl.BlockSpec(memory_space=pl.ANY)


def window_of(mask_hbm, target_hbm, mask_window, target_window, sems, share, margin):
    rows, clip_cols = mask_hbm.shape
    loaded = mask_window.shape[1]
    width = loaded - 128
    start = lax.axis_index("kern") * share - 2 * margin
    base = (start + 128) // 128 * 128 - 128
    base = jnp.minimum(jnp.maximum(base, 0), clip_cols - loaded)
    base = pl.multiple_of(base, 128)
    loads = [
        pltpu.make_async_copy(mask_hbm.at[:, pl.ds(base, loaded)], mask_window, sems.at[0]),
        pltpu.make_async_copy(target_hbm.at[:, pl.ds(base, loaded)], target_window, sems.at[1]),
    ]

    def finish():
        for load in loads:
            load.wait()
        clip_col = start + lax.broadcasted_iota(jnp.int32, (rows, width), 1)
        col_inside = jnp.logical_and(clip_col >= 0, clip_col < clip_cols)
        back = lax.rem(base - start + loaded, loaded)
        mask_own = pltpu.roll(mask_window[...], back, 1)[:, :width]
        mask_own = jnp.where(col_inside, mask_own, 0.0).astype(jnp.bfloat16)
        target_own = pltpu.roll(target_window[...].astype(jnp.float32), back, 1)[:, :width]
        return mask_own, target_own.astype(jnp.bfloat16)

    return loads, finish


def exchange_kernel(
    sizes, mask_hbm, target_hbm, kernel_hbm, assign_hbm, all_taps, above, below,
    mask_window, target_window, send_up, send_down, square, tap_rows, own_taps, kernel_ref,
    assign_own, load_sem, own_sem, tap_send, tap_recv, halo_send, halo_recv,
):
    kern_count, tile_count, span, share = sizes
    tile = lax.axis_index("tile")
    kern = lax.axis_index("kern")
    rows = mask_hbm.shape[0]
    margin = (span - 1) // 2
    depth = -(-span * PITCH // 128) * 128
    has_up = tile > 0
    has_down = tile < tile_count - 1

    barrier = pltpu.get_barrier_semaphore()
    for step in range(1, kern_count):
        peer = lax.rem(kern + step, kern_count)
        pl.semaphore_signal(barrier, inc=1, device_id=(tile, peer), device_id_type=MESH)

    @pl.when(has_up)
    def _():
        pl.semaphore_signal(barrier, inc=1, device_id=(tile - 1, kern), device_id_type=MESH)

    @pl.when(has_down)
    def _():
        pl.semaphore_signal(barrier, inc=1, device_id=(tile + 1, kern), device_id_type=MESH)

    small_loads = [
        pltpu.make_async_copy(kernel_hbm, kernel_ref, load_sem.at[2]),
        pltpu.make_async_copy(assign_hbm, assign_own, load_sem.at[3]),
    ]
    loads, finish = window_of(
        mask_hbm, target_hbm, mask_window, target_window, load_sem, share, margin
    )
    for load in small_loads + loads:
        load.start()

    square[...] = jnp.zeros_like(square)
    for load in small_loads:
        load.wait()
    for row in range(span):
        pair = kernel_ref[row].astype(jnp.float32)
        square[0, row : row + 1, 0:span] = pair[0:1]
        square[1, row : row + 1, 0:span] = pair[1:2]
    lane = lax.broadcasted_iota(jnp.int32, (1, 128), 1)
    chunk_count = depth // 128
    for part in range(2):
        turned = square[part].T
        chunks = [jnp.zeros((1, 128), jnp.float32)] * chunk_count
        for column in range(span):
            chunk, offset = divmod(column * PITCH, 128)
            row = turned[column : column + 1]
            row = pltpu.roll(row, offset, 1) if offset else row
            if offset + span <= 128:
                chunks[chunk] = chunks[chunk] + row
            else:
                chunks[chunk] = chunks[chunk] + jnp.where(lane >= offset, row, 0.0)
                chunks[chunk + 1] = chunks[chunk + 1] + jnp.where(lane < offset, row, 0.0)
        mark = assign_own[0].astype(jnp.float32)
        chunks[-1] = jnp.where(lane >= 112, mark, chunks[-1])
        for chunk in range(chunk_count):
            tap_rows[8 * part + chunk : 8 * part + chunk + 1, :] = chunks[chunk]
    own_taps[...] = tap_rows[...].astype(jnp.bfloat16)

    own_copy = pltpu.make_async_copy(own_taps, all_taps.at[0], own_sem)
    own_copy.start()
    upward = pltpu.make_async_remote_copy(
        src_ref=send_up,
        dst_ref=below,
        send_sem=halo_send.at[0],
        recv_sem=halo_recv.at[0],
        device_id=(tile - 1, kern),
        device_id_type=MESH,
    )
    downward = pltpu.make_async_remote_copy(
        src_ref=send_down,
        dst_ref=above,
        send_sem=halo_send.at[1],
        recv_sem=halo_recv.at[1],
        device_id=(tile + 1, kern),
        device_id_type=MESH,
    )
    pl.semaphore_wait(barrier, kern_count - 1 + has_up.astype(jnp.int32) + has_down.astype(jnp.int32))
    tap_copies = []
    for step in range(1, kern_count):
        peer = lax.rem(kern + step, kern_count)
        tap_copies.append(
            pltpu.make_async_remote_copy(
                src_ref=own_taps,
                dst_ref=all_taps.at[step],
                send_sem=tap_send.at[step],
                recv_sem=tap_recv.at[step],
                device_id=(tile, peer),
                device_id_type=MESH,
            )
        )
    for copy in tap_copies:
        copy.start()
    mask_own, target_own = finish()
    send_up[0:MASK_HALO, :] = mask_own[0:MASK_HALO]
    send_up[MASK_HALO:, :] = target_own[0:TARGET_HALO]
    send_down[0:MASK_HALO, :] = mask_own[rows - MASK_HALO :]
    send_down[MASK_HALO:, :] = target_own[rows - TARGET_HALO :]
    pl.when(has_up)(upward.start)
    pl.when(has_down)(downward.start)
    own_copy.wait()
    for copy in tap_copies:
        copy.wait()
    pl.when(has_up)(upward.wait_send)
    pl.when(has_down)(downward.wait_send)
    pl.when(has_up)(downward.wait_recv)
    pl.when(has_down)(upward.wait_recv)


def gradient_kernel(
    sizes, mask_hbm, target_hbm, weight_hbm, taps_hbm, above_hbm, below_hbm, grad_out, resist_out,
    mask_window, target_window, weight_ref, all_taps, above, below, mask_rows, target_rows, toeplitz,
    shifted, fields, adjoint, spread, resist_rows, grad_rows, resist_own, grad_own, flipped, resist_wide,
    load_sem, store_sem,
):
    kern_count, tile_count, span, share = sizes
    tile = lax.axis_index("tile")
    kern = lax.axis_index("kern")
    rows, clip_cols = mask_hbm.shape
    clip_rows = rows * tile_count
    margin = (span - 1) // 2
    height = (rows + 2 * margin) // BLOCKS
    padded = -(-height // 16) * 16
    depth = toeplitz.shape[1]
    chunk_count = depth // 128
    reach = share + 4 * margin
    width = above.shape[1]
    lanes = shifted.shape[1]

    loads, finish = window_of(
        mask_hbm, target_hbm, mask_window, target_window, load_sem, share, margin
    )
    halo_loads = [
        pltpu.make_async_copy(above_hbm, above, load_sem.at[2]),
        pltpu.make_async_copy(below_hbm, below, load_sem.at[3]),
    ]
    tap_loads = [
        pltpu.make_async_copy(taps_hbm, all_taps, load_sem.at[4]),
        pltpu.make_async_copy(weight_hbm, weight_ref, load_sem.at[5]),
    ]
    for load in loads + halo_loads + tap_loads:
        load.start()

    mask_own, target_own = finish()
    mask_rows[MASK_HALO : MASK_HALO + rows, :] = mask_own.astype(jnp.float32)
    target_rows[TARGET_HALO : TARGET_HALO + rows, :] = target_own.astype(jnp.float32)
    for load in halo_loads:
        load.wait()
    for halo, inside, mask_at, target_at in (
        (above, tile > 0, 0, 0),
        (below, tile < tile_count - 1, MASK_HALO + rows, TARGET_HALO + rows),
    ):
        held = jnp.where(inside, halo[...].astype(jnp.float32), 0.0)
        mask_rows[mask_at : mask_at + MASK_HALO, :] = held[0:MASK_HALO]
        target_rows[target_at : target_at + TARGET_HALO, :] = held[MASK_HALO:]

    def side_by_side(held, top, count, shift):
        pieces = []
        for block in range(BLOCKS):
            piece = held[top + block * height : top + block * height + count, :]
            piece = pltpu.roll(piece, width - shift, 1) if shift else piece
            pieces.append(piece[:, :reach])
        if lanes > BLOCKS * reach:
            pieces.append(jnp.zeros((count, lanes - BLOCKS * reach), jnp.float32))
        return jnp.concatenate(pieces, axis=1)

    window = side_by_side(mask_rows, MASK_HALO - 2 * margin, PITCH, 0)
    for column in range(span):
        turned = window if column == 0 else pltpu.roll(window, lanes - column, 1)
        shifted[column * PITCH : (column + 1) * PITCH, :] = turned.astype(jnp.bfloat16)
    shifted[span * PITCH :, :] = jnp.zeros((depth - span * PITCH, lanes), jnp.bfloat16)

    for load in tap_loads:
        load.wait()
    weights = weight_ref[...]
    total = jnp.sum(weights, axis=1, keepdims=True)
    slot_ids = lax.broadcasted_iota(jnp.int32, weights.shape, 1).astype(jnp.float32)
    own_lane = lax.broadcasted_iota(jnp.int32, (padded, 128), 1)
    own_row = lax.broadcasted_iota(jnp.int32, (padded, 128), 0)
    same_chunk = own_lane >= own_row
    shares = []
    for source in range(kern_count):
        block = all_taps[source].astype(jnp.float32)
        picked = jnp.where(slot_ids == block[7:8, 112:113], weights, 0.0)
        shares.append(jnp.sum(picked, axis=1, keepdims=True) / total)
        for part in range(2):
            first = (2 * source + part) * padded
            before = jnp.zeros((padded, 128), jnp.float32)
            for chunk in range(chunk_count):
                at = 8 * part + chunk
                row = jnp.broadcast_to(block[at : at + 1], (padded, 128))
                turned = pltpu.roll(row, 0, 1, stride=1, stride_axis=0)
                toeplitz[first : first + padded, chunk * 128 : (chunk + 1) * 128] = jnp.where(
                    same_chunk, turned, before
                ).astype(jnp.bfloat16)
                before = turned

    flipped[...] = toeplitz[...].T
    target = side_by_side(target_rows, TARGET_HALO - margin, padded, margin)
    for tile_at in range(0, lanes, 256):
        tile_lanes = slice(tile_at, min(tile_at + 256, lanes))
        count = min(256, lanes - tile_at)
        fields[:, tile_lanes] = jnp.dot(
            toeplitz[...], shifted[:, tile_lanes], preferred_element_type=jnp.float32
        )
        row_at = lax.broadcasted_iota(jnp.int32, (padded, count), 0)
        col_at = lax.broadcasted_iota(jnp.int32, (padded, count), 1) + tile_at
        clip_row = tile * rows - margin + row_at
        clip_col = kern * share - margin + col_at
        for block in range(1, BLOCKS):
            later = col_at >= block * reach
            clip_row = jnp.where(later, clip_row + height, clip_row)
            clip_col = jnp.where(later, clip_col - reach, clip_col)
        inside = jnp.logical_and(
            jnp.logical_and(clip_row >= 0, clip_row < clip_rows),
            jnp.logical_and(clip_col >= 0, clip_col < clip_cols),
        )
        inside = jnp.logical_and(inside, row_at < height)
        aerial = jnp.zeros((padded, count), jnp.float32)
        for source in range(kern_count):
            first = 2 * source * padded
            real = fields[first : first + padded, tile_lanes]
            imag = fields[first + padded : first + 2 * padded, tile_lanes]
            aerial = aerial + shares[source] * (real * real + imag * imag)
        resist = 1.0 / (1.0 + jnp.exp(-SLOPE_FACTOR * (aerial - LEVEL_VALUE)))
        resist_wide[:, tile_lanes] = resist
        sense = 2.0 * (resist - target[:, tile_lanes]) * SLOPE_FACTOR * resist * (1.0 - resist)
        sense = jnp.where(inside, sense, 0.0)
        for source in range(kern_count):
            scaled = (2.0 * shares[source]) * sense
            for part in range(2):
                first = (2 * source + part) * padded
                adjoint[first : first + padded, tile_lanes] = (
                    scaled * fields[first : first + padded, tile_lanes]
                ).astype(jnp.bfloat16)
        spread[:, tile_lanes] = jnp.dot(
            flipped[...], adjoint[:, tile_lanes], preferred_element_type=jnp.float32
        )
    resist = resist_wide[...]
    for block in range(BLOCKS):
        piece = pltpu.roll(resist, lanes - block * reach - margin, 1)[:, :share]
        resist_rows[block * height : block * height + padded, :] = piece
    resist_own[...] = resist_rows[margin : margin + rows, :]
    resist_store = pltpu.make_async_copy(resist_own, resist_out, store_sem.at[0])
    resist_store.start()

    gathered = spread[0:PITCH, :]
    for column in range(1, span):
        place = column * PITCH
        gathered = gathered + pltpu.roll(spread[place : place + PITCH, :], column, 1)
    grad_rows[...] = jnp.zeros_like(grad_rows)
    for block in range(BLOCKS):
        piece = pltpu.roll(gathered, lanes - block * reach - 2 * margin, 1)[:, :share]
        grad_rows[block * height : block * height + PITCH, :] += piece
    grad_own[...] = grad_rows[2 * margin : 2 * margin + rows, :]
    grad_store = pltpu.make_async_copy(grad_own, grad_out, store_sem.at[1])
    grad_store.start()

    resist_store.wait()
    grad_store.wait()


def on_device(mask, target, kernels, source_weight, assign):
    rows, col_count = mask.shape
    span = kernels.shape[-1]
    margin = (span - 1) // 2
    kern_count = lax.axis_size("kern")
    tile_count = lax.axis_size("tile")
    share = col_count // kern_count
    reach = share + 4 * margin
    width = -(-reach // 128) * 128
    lanes = -(-BLOCKS * reach // 128) * 128
    depth = -(-span * PITCH // 128) * 128
    height = (rows + 2 * margin) // BLOCKS
    padded = -(-height // 16) * 16
    parts = 2 * kern_count
    halo = MASK_HALO + TARGET_HALO
    sizes = (kern_count, tile_count, span, share)
    limit = 56 * 1024 * 1024
    by_row = jnp.swapaxes(kernels[0], 0, 1)
    taps, above, below = pl.pallas_call(
        functools.partial(exchange_kernel, sizes),
        out_shape=(
            jax.ShapeDtypeStruct((kern_count, 16, 128), jnp.bfloat16),
            jax.ShapeDtypeStruct((halo, width), jnp.bfloat16),
            jax.ShapeDtypeStruct((halo, width), jnp.bfloat16),
        ),
        in_specs=[IN_ANY] * 4,
        out_specs=(IN_ANY,) * 3,
        scratch_shapes=[
            pltpu.VMEM((rows, width + 128), jnp.float32),
            pltpu.VMEM((rows, width + 128), jnp.int32),
            pltpu.VMEM((halo, width), jnp.bfloat16),
            pltpu.VMEM((halo, width), jnp.bfloat16),
            pltpu.VMEM((2, 128, 128), jnp.float32),
            pltpu.VMEM((16, 128), jnp.float32),
            pltpu.VMEM((16, 128), jnp.bfloat16),
            pltpu.VMEM(by_row.shape, by_row.dtype),
            pltpu.SMEM((1,), jnp.int32),
            pltpu.SemaphoreType.DMA((4,)),
            pltpu.SemaphoreType.DMA,
            pltpu.SemaphoreType.DMA((kern_count,)),
            pltpu.SemaphoreType.DMA((kern_count,)),
            pltpu.SemaphoreType.DMA((2,)),
            pltpu.SemaphoreType.DMA((2,)),
        ],
        compiler_params=pltpu.CompilerParams(
            collective_id=0, has_side_effects=True, vmem_limit_bytes=limit
        ),
        name="exchange",
    )(mask, target, by_row, assign)
    image = jax.ShapeDtypeStruct((rows, share), jnp.float32)
    return pl.pallas_call(
        functools.partial(gradient_kernel, sizes),
        out_shape=(image, image),
        in_specs=[IN_ANY] * 6,
        out_specs=(IN_ANY, IN_ANY),
        scratch_shapes=[
            pltpu.VMEM((rows, width + 128), jnp.float32),
            pltpu.VMEM((rows, width + 128), jnp.int32),
            pltpu.VMEM((1, source_weight.shape[0]), jnp.float32),
            pltpu.VMEM((kern_count, 16, 128), jnp.bfloat16),
            pltpu.VMEM((halo, width), jnp.bfloat16),
            pltpu.VMEM((halo, width), jnp.bfloat16),
            pltpu.VMEM((rows + 2 * MASK_HALO, width), jnp.float32),
            pltpu.VMEM((rows + 2 * TARGET_HALO, width), jnp.float32),
            pltpu.VMEM((parts * padded, depth), jnp.bfloat16),
            pltpu.VMEM((depth, lanes), jnp.bfloat16),
            pltpu.VMEM((parts * padded, lanes), jnp.float32),
            pltpu.VMEM((parts * padded, lanes), jnp.bfloat16),
            pltpu.VMEM((depth, lanes), jnp.float32),
            pltpu.VMEM(((BLOCKS - 1) * height + padded, share), jnp.float32),
            pltpu.VMEM(((BLOCKS - 1) * height + PITCH, share), jnp.float32),
            pltpu.VMEM((rows, share), jnp.float32),
            pltpu.VMEM((rows, share), jnp.float32),
            pltpu.VMEM((depth, parts * padded), jnp.bfloat16),
            pltpu.VMEM((padded, lanes), jnp.float32),
            pltpu.SemaphoreType.DMA((6,)),
            pltpu.SemaphoreType.DMA((2,)),
        ],
        compiler_params=pltpu.CompilerParams(vmem_limit_bytes=limit),
        name="image_gradient",
    )(mask, target, source_weight[None, :], taps, above, below)


def solution(mesh):
    placed = (P("tile", None), P("tile", None), P("kern", None, None, None), P(), P("kern"))
    return jax.shard_map(
        on_device,
        mesh=mesh,
        in_specs=placed,
        out_specs=(P("tile", "kern"), P("tile", "kern")),
        check_vma=False,
    )
```

```python
import functools

import jax
import jax.numpy as jnp
from jax import lax
from jax.experimental import pallas as pl
from jax.experimental.pallas import tpu as pltpu
from jax.sharding import PartitionSpec as P

SLOPE_FACTOR = 4.0
LEVEL_VALUE = 0.6
BLOCKS = 3
PITCH = 48
MASK_HALO = 32
TARGET_HALO = 16
MESH = pl.DeviceIdType.MESH
IN_VMEM = pl.BlockSpec(memory_space=pltpu.VMEM)
IN_ANY = pl.BlockSpec(memory_space=pl.ANY)


def window_of(mask_hbm, target_hbm, mask_window, target_window, sems, share, margin):
    rows, clip_cols = mask_hbm.shape
    loaded = mask_window.shape[1]
    width = loaded - 128
    start = lax.axis_index("kern") * share - 2 * margin
    base = (start + 128) // 128 * 128 - 128
    base = jnp.minimum(jnp.maximum(base, 0), clip_cols - loaded)
    base = pl.multiple_of(base, 128)
    loads = [
        pltpu.make_async_copy(mask_hbm.at[:, pl.ds(base, loaded)], mask_window, sems.at[0]),
        pltpu.make_async_copy(target_hbm.at[:, pl.ds(base, loaded)], target_window, sems.at[1]),
    ]

    def finish():
        for load in loads:
            load.wait()
        clip_col = start + lax.broadcasted_iota(jnp.int32, (rows, width), 1)
        col_inside = jnp.logical_and(clip_col >= 0, clip_col < clip_cols)
        back = lax.rem(base - start + loaded, loaded)
        mask_own = pltpu.roll(mask_window[...], back, 1)[:, :width]
        mask_own = jnp.where(col_inside, mask_own, 0.0).astype(jnp.bfloat16)
        target_own = pltpu.roll(target_window[...].astype(jnp.float32), back, 1)[:, :width]
        return mask_own, target_own.astype(jnp.bfloat16)

    return loads, finish


def exchange_kernel(
    sizes, mask_hbm, target_hbm, kernel_hbm, assign_hbm, all_taps, above, below,
    mask_window, target_window, send_up, send_down, square, tap_rows, own_taps, kernel_ref,
    assign_own, load_sem, own_sem, tap_send, tap_recv, halo_send, halo_recv,
):
    kern_count, tile_count, span, share = sizes
    tile = lax.axis_index("tile")
    kern = lax.axis_index("kern")
    rows = mask_hbm.shape[0]
    margin = (span - 1) // 2
    depth = -(-span * PITCH // 128) * 128
    has_up = tile > 0
    has_down = tile < tile_count - 1

    barrier = pltpu.get_barrier_semaphore()
    for step in range(1, kern_count):
        peer = lax.rem(kern + step, kern_count)
        pl.semaphore_signal(barrier, inc=1, device_id=(tile, peer), device_id_type=MESH)

    @pl.when(has_up)
    def _():
        pl.semaphore_signal(barrier, inc=1, device_id=(tile - 1, kern), device_id_type=MESH)

    @pl.when(has_down)
    def _():
        pl.semaphore_signal(barrier, inc=1, device_id=(tile + 1, kern), device_id_type=MESH)

    small_loads = [
        pltpu.make_async_copy(kernel_hbm, kernel_ref, load_sem.at[2]),
        pltpu.make_async_copy(assign_hbm, assign_own, load_sem.at[3]),
    ]
    loads, finish = window_of(
        mask_hbm, target_hbm, mask_window, target_window, load_sem, share, margin
    )
    for load in small_loads + loads:
        load.start()

    square[...] = jnp.zeros_like(square)
    for load in small_loads:
        load.wait()
    for row in range(span):
        pair = kernel_ref[row].astype(jnp.float32)
        square[0, row : row + 1, 0:span] = pair[0:1]
        square[1, row : row + 1, 0:span] = pair[1:2]
    lane = lax.broadcasted_iota(jnp.int32, (1, 128), 1)
    chunk_count = depth // 128
    for part in range(2):
        turned = square[part].T
        chunks = [jnp.zeros((1, 128), jnp.float32)] * chunk_count
        for column in range(span):
            chunk, offset = divmod(column * PITCH, 128)
            row = turned[column : column + 1]
            row = pltpu.roll(row, offset, 1) if offset else row
            if offset + span <= 128:
                chunks[chunk] = chunks[chunk] + row
            else:
                chunks[chunk] = chunks[chunk] + jnp.where(lane >= offset, row, 0.0)
                chunks[chunk + 1] = chunks[chunk + 1] + jnp.where(lane < offset, row, 0.0)
        mark = assign_own[0].astype(jnp.float32)
        chunks[-1] = jnp.where(lane >= 112, mark, chunks[-1])
        for chunk in range(chunk_count):
            tap_rows[8 * part + chunk : 8 * part + chunk + 1, :] = chunks[chunk]
    own_taps[...] = tap_rows[...].astype(jnp.bfloat16)

    own_copy = pltpu.make_async_copy(own_taps, all_taps.at[0], own_sem)
    own_copy.start()
    upward = pltpu.make_async_remote_copy(
        src_ref=send_up,
        dst_ref=below,
        send_sem=halo_send.at[0],
        recv_sem=halo_recv.at[0],
        device_id=(tile - 1, kern),
        device_id_type=MESH,
    )
    downward = pltpu.make_async_remote_copy(
        src_ref=send_down,
        dst_ref=above,
        send_sem=halo_send.at[1],
        recv_sem=halo_recv.at[1],
        device_id=(tile + 1, kern),
        device_id_type=MESH,
    )
    pl.semaphore_wait(barrier, kern_count - 1 + has_up.astype(jnp.int32) + has_down.astype(jnp.int32))
    tap_copies = []
    for step in range(1, kern_count):
        peer = lax.rem(kern + step, kern_count)
        tap_copies.append(
            pltpu.make_async_remote_copy(
                src_ref=own_taps,
                dst_ref=all_taps.at[step],
                send_sem=tap_send.at[step],
                recv_sem=tap_recv.at[step],
                device_id=(tile, peer),
                device_id_type=MESH,
            )
        )
    for copy in tap_copies:
        copy.start()
    mask_own, target_own = finish()
    send_up[0:MASK_HALO, :] = mask_own[0:MASK_HALO]
    send_up[MASK_HALO:, :] = target_own[0:TARGET_HALO]
    send_down[0:MASK_HALO, :] = mask_own[rows - MASK_HALO :]
    send_down[MASK_HALO:, :] = target_own[rows - TARGET_HALO :]
    pl.when(has_up)(upward.start)
    pl.when(has_down)(downward.start)
    own_copy.wait()
    for copy in tap_copies:
        copy.wait()
    pl.when(has_up)(upward.wait_send)
    pl.when(has_down)(downward.wait_send)
    pl.when(has_up)(downward.wait_recv)
    pl.when(has_down)(upward.wait_recv)


def gradient_kernel(
    sizes, mask_hbm, target_hbm, weight_hbm, taps_hbm, above_hbm, below_hbm, grad_out, resist_out,
    mask_window, target_window, weight_ref, all_taps, above, below, mask_rows, target_rows, toeplitz,
    shifted, fields, adjoint, spread, resist_rows, grad_rows, resist_own, grad_own, flipped,
    load_sem, store_sem,
):
    kern_count, tile_count, span, share = sizes
    tile = lax.axis_index("tile")
    kern = lax.axis_index("kern")
    rows, clip_cols = mask_hbm.shape
    clip_rows = rows * tile_count
    margin = (span - 1) // 2
    height = (rows + 2 * margin) // BLOCKS
    padded = -(-height // 16) * 16
    depth = toeplitz.shape[1]
    chunk_count = depth // 128
    reach = share + 4 * margin
    width = above.shape[1]
    lanes = shifted.shape[1]

    loads, finish = window_of(
        mask_hbm, target_hbm, mask_window, target_window, load_sem, share, margin
    )
    halo_loads = [
        pltpu.make_async_copy(above_hbm, above, load_sem.at[2]),
        pltpu.make_async_copy(below_hbm, below, load_sem.at[3]),
    ]
    tap_loads = [
        pltpu.make_async_copy(taps_hbm, all_taps, load_sem.at[4]),
        pltpu.make_async_copy(weight_hbm, weight_ref, load_sem.at[5]),
    ]
    for load in loads + halo_loads + tap_loads:
        load.start()

    mask_own, target_own = finish()
    mask_rows[MASK_HALO : MASK_HALO + rows, :] = mask_own.astype(jnp.float32)
    target_rows[TARGET_HALO : TARGET_HALO + rows, :] = target_own.astype(jnp.float32)
    for load in halo_loads:
        load.wait()
    for halo, inside, mask_at, target_at in (
        (above, tile > 0, 0, 0),
        (below, tile < tile_count - 1, MASK_HALO + rows, TARGET_HALO + rows),
    ):
        held = jnp.where(inside, halo[...].astype(jnp.float32), 0.0)
        mask_rows[mask_at : mask_at + MASK_HALO, :] = held[0:MASK_HALO]
        target_rows[target_at : target_at + TARGET_HALO, :] = held[MASK_HALO:]

    def side_by_side(held, top, count, shift):
        pieces = []
        for block in range(BLOCKS):
            piece = held[top + block * height : top + block * height + count, :]
            piece = pltpu.roll(piece, width - shift, 1) if shift else piece
            pieces.append(piece[:, :reach])
        if lanes > BLOCKS * reach:
            pieces.append(jnp.zeros((count, lanes - BLOCKS * reach), jnp.float32))
        return jnp.concatenate(pieces, axis=1)

    window = side_by_side(mask_rows, MASK_HALO - 2 * margin, PITCH, 0)
    for column in range(span):
        turned = window if column == 0 else pltpu.roll(window, lanes - column, 1)
        shifted[column * PITCH : (column + 1) * PITCH, :] = turned.astype(jnp.bfloat16)
    shifted[span * PITCH :, :] = jnp.zeros((depth - span * PITCH, lanes), jnp.bfloat16)

    for load in tap_loads:
        load.wait()
    weights = weight_ref[...]
    total = jnp.sum(weights, axis=1, keepdims=True)
    slot_ids = lax.broadcasted_iota(jnp.int32, weights.shape, 1).astype(jnp.float32)
    own_lane = lax.broadcasted_iota(jnp.int32, (padded, 128), 1)
    own_row = lax.broadcasted_iota(jnp.int32, (padded, 128), 0)
    same_chunk = own_lane >= own_row
    shares = []
    for source in range(kern_count):
        block = all_taps[source].astype(jnp.float32)
        picked = jnp.where(slot_ids == block[7:8, 112:113], weights, 0.0)
        shares.append(jnp.sum(picked, axis=1, keepdims=True) / total)
        for part in range(2):
            first = (2 * source + part) * padded
            before = jnp.zeros((padded, 128), jnp.float32)
            for chunk in range(chunk_count):
                at = 8 * part + chunk
                row = jnp.broadcast_to(block[at : at + 1], (padded, 128))
                turned = pltpu.roll(row, 0, 1, stride=1, stride_axis=0)
                toeplitz[first : first + padded, chunk * 128 : (chunk + 1) * 128] = jnp.where(
                    same_chunk, turned, before
                ).astype(jnp.bfloat16)
                before = turned

    flipped[...] = toeplitz[...].T
    fields[...] = jnp.dot(toeplitz[...], shifted[...], preferred_element_type=jnp.float32)

    row_at = lax.broadcasted_iota(jnp.int32, (padded, lanes), 0)
    col_at = lax.broadcasted_iota(jnp.int32, (padded, lanes), 1)
    clip_row = tile * rows - margin + row_at
    clip_col = kern * share - margin + col_at
    for block in range(1, BLOCKS):
        later = col_at >= block * reach
        clip_row = jnp.where(later, clip_row + height, clip_row)
        clip_col = jnp.where(later, clip_col - reach, clip_col)
    inside = jnp.logical_and(
        jnp.logical_and(clip_row >= 0, clip_row < clip_rows),
        jnp.logical_and(clip_col >= 0, clip_col < clip_cols),
    )
    inside = jnp.logical_and(inside, row_at < height)
    target = side_by_side(target_rows, TARGET_HALO - margin, padded, margin)
    aerial = jnp.zeros((padded, lanes), jnp.float32)
    for source in range(kern_count):
        first = 2 * source * padded
        real = fields[first : first + padded, :]
        imag = fields[first + padded : first + 2 * padded, :]
        aerial = aerial + shares[source] * (real * real + imag * imag)
    resist = 1.0 / (1.0 + jnp.exp(-SLOPE_FACTOR * (aerial - LEVEL_VALUE)))
    sense = 2.0 * (resist - target) * SLOPE_FACTOR * resist * (1.0 - resist)
    sense = jnp.where(inside, sense, 0.0)
    for source in range(kern_count):
        scaled = (2.0 * shares[source]) * sense
        for part in range(2):
            first = (2 * source + part) * padded
            adjoint[first : first + padded, :] = (
                scaled * fields[first : first + padded, :]
            ).astype(jnp.bfloat16)
    for block in range(BLOCKS):
        piece = pltpu.roll(resist, lanes - block * reach - margin, 1)[:, :share]
        resist_rows[block * height : block * height + padded, :] = piece
    resist_own[...] = resist_rows[margin : margin + rows, :]
    resist_store = pltpu.make_async_copy(resist_own, resist_out, store_sem.at[0])
    resist_store.start()

    spread[...] = jnp.dot(flipped[...], adjoint[...], preferred_element_type=jnp.float32)

    gathered = spread[0:PITCH, :]
    for column in range(1, span):
        place = column * PITCH
        gathered = gathered + pltpu.roll(spread[place : place + PITCH, :], column, 1)
    grad_rows[...] = jnp.zeros_like(grad_rows)
    for block in range(BLOCKS):
        piece = pltpu.roll(gathered, lanes - block * reach - 2 * margin, 1)[:, :share]
        grad_rows[block * height : block * height + PITCH, :] += piece
    grad_own[...] = grad_rows[2 * margin : 2 * margin + rows, :]
    grad_store = pltpu.make_async_copy(grad_own, grad_out, store_sem.at[1])
    grad_store.start()

    resist_store.wait()
    grad_store.wait()


def on_device(mask, target, kernels, source_weight, assign):
    rows, col_count = mask.shape
    span = kernels.shape[-1]
    margin = (span - 1) // 2
    kern_count = lax.axis_size("kern")
    tile_count = lax.axis_size("tile")
    share = col_count // kern_count
    reach = share + 4 * margin
    width = -(-reach // 128) * 128
    lanes = -(-BLOCKS * reach // 128) * 128
    depth = -(-span * PITCH // 128) * 128
    height = (rows + 2 * margin) // BLOCKS
    padded = -(-height // 16) * 16
    parts = 2 * kern_count
    halo = MASK_HALO + TARGET_HALO
    sizes = (kern_count, tile_count, span, share)
    limit = 56 * 1024 * 1024
    by_row = jnp.swapaxes(kernels[0], 0, 1)
    taps, above, below = pl.pallas_call(
        functools.partial(exchange_kernel, sizes),
        out_shape=(
            jax.ShapeDtypeStruct((kern_count, 16, 128), jnp.bfloat16),
            jax.ShapeDtypeStruct((halo, width), jnp.bfloat16),
            jax.ShapeDtypeStruct((halo, width), jnp.bfloat16),
        ),
        in_specs=[IN_ANY] * 4,
        out_specs=(IN_ANY,) * 3,
        scratch_shapes=[
            pltpu.VMEM((rows, width + 128), jnp.float32),
            pltpu.VMEM((rows, width + 128), jnp.int32),
            pltpu.VMEM((halo, width), jnp.bfloat16),
            pltpu.VMEM((halo, width), jnp.bfloat16),
            pltpu.VMEM((2, 128, 128), jnp.float32),
            pltpu.VMEM((16, 128), jnp.float32),
            pltpu.VMEM((16, 128), jnp.bfloat16),
            pltpu.VMEM(by_row.shape, by_row.dtype),
            pltpu.SMEM((1,), jnp.int32),
            pltpu.SemaphoreType.DMA((4,)),
            pltpu.SemaphoreType.DMA,
            pltpu.SemaphoreType.DMA((kern_count,)),
            pltpu.SemaphoreType.DMA((kern_count,)),
            pltpu.SemaphoreType.DMA((2,)),
            pltpu.SemaphoreType.DMA((2,)),
        ],
        compiler_params=pltpu.CompilerParams(
            collective_id=0, has_side_effects=True, vmem_limit_bytes=limit
        ),
        name="exchange",
    )(mask, target, by_row, assign)
    image = jax.ShapeDtypeStruct((rows, share), jnp.float32)
    return pl.pallas_call(
        functools.partial(gradient_kernel, sizes),
        out_shape=(image, image),
        in_specs=[IN_ANY] * 6,
        out_specs=(IN_ANY, IN_ANY),
        scratch_shapes=[
            pltpu.VMEM((rows, width + 128), jnp.float32),
            pltpu.VMEM((rows, width + 128), jnp.int32),
            pltpu.VMEM((1, source_weight.shape[0]), jnp.float32),
            pltpu.VMEM((kern_count, 16, 128), jnp.bfloat16),
            pltpu.VMEM((halo, width), jnp.bfloat16),
            pltpu.VMEM((halo, width), jnp.bfloat16),
            pltpu.VMEM((rows + 2 * MASK_HALO, width), jnp.float32),
            pltpu.VMEM((rows + 2 * TARGET_HALO, width), jnp.float32),
            pltpu.VMEM((parts * padded, depth), jnp.bfloat16),
            pltpu.VMEM((depth, lanes), jnp.bfloat16),
            pltpu.VMEM((parts * padded, lanes), jnp.float32),
            pltpu.VMEM((parts * padded, lanes), jnp.bfloat16),
            pltpu.VMEM((depth, lanes), jnp.float32),
            pltpu.VMEM(((BLOCKS - 1) * height + padded, share), jnp.float32),
            pltpu.VMEM(((BLOCKS - 1) * height + PITCH, share), jnp.float32),
            pltpu.VMEM((rows, share), jnp.float32),
            pltpu.VMEM((rows, share), jnp.float32),
            pltpu.VMEM((depth, parts * padded), jnp.bfloat16),
            pltpu.SemaphoreType.DMA((6,)),
            pltpu.SemaphoreType.DMA((2,)),
        ],
        compiler_params=pltpu.CompilerParams(vmem_limit_bytes=limit),
        name="image_gradient",
    )(mask, target, source_weight[None, :], taps, above, below)


def solution(mesh):
    placed = (P("tile", None), P("tile", None), P("kern", None, None, None), P(), P("kern"))
    return jax.shard_map(
        on_device,
        mesh=mesh,
        in_specs=placed,
        out_specs=(P("tile", "kern"), P("tile", "kern")),
        check_vma=False,
    )
```

```python
import functools

import jax
import jax.numpy as jnp
from jax import lax
from jax.experimental import pallas as pl
from jax.experimental.pallas import tpu as pltpu
from jax.sharding import PartitionSpec as P

SLOPE_FACTOR = 4.0
LEVEL_VALUE = 0.6
BLOCKS = 3
PITCH = 48
MASK_HALO = 32
TARGET_HALO = 16
MESH = pl.DeviceIdType.MESH
IN_VMEM = pl.BlockSpec(memory_space=pltpu.VMEM)
IN_ANY = pl.BlockSpec(memory_space=pl.ANY)


def window_of(mask_hbm, target_hbm, mask_window, target_window, sems, share, margin):
    rows, clip_cols = mask_hbm.shape
    loaded = mask_window.shape[1]
    width = loaded - 128
    start = lax.axis_index("kern") * share - 2 * margin
    base = (start + 128) // 128 * 128 - 128
    base = jnp.minimum(jnp.maximum(base, 0), clip_cols - loaded)
    base = pl.multiple_of(base, 128)
    loads = [
        pltpu.make_async_copy(mask_hbm.at[:, pl.ds(base, loaded)], mask_window, sems.at[0]),
        pltpu.make_async_copy(target_hbm.at[:, pl.ds(base, loaded)], target_window, sems.at[1]),
    ]

    def finish():
        for load in loads:
            load.wait()
        clip_col = start + lax.broadcasted_iota(jnp.int32, (rows, width), 1)
        col_inside = jnp.logical_and(clip_col >= 0, clip_col < clip_cols)
        back = lax.rem(base - start + loaded, loaded)
        mask_own = pltpu.roll(mask_window[...], back, 1)[:, :width]
        mask_own = jnp.where(col_inside, mask_own, 0.0).astype(jnp.bfloat16)
        target_own = pltpu.roll(target_window[...].astype(jnp.float32), back, 1)[:, :width]
        return mask_own, target_own.astype(jnp.bfloat16)

    return loads, finish


def exchange_kernel(
    sizes, mask_hbm, target_hbm, kernel_hbm, assign_hbm, all_taps, above, below, own_rows,
    mask_window, target_window, send_up, send_down, square, tap_rows, own_taps, kernel_ref,
    assign_own, own_image, load_sem, own_sem, tap_send, tap_recv, halo_send, halo_recv,
):
    kern_count, tile_count, span, share = sizes
    tile = lax.axis_index("tile")
    kern = lax.axis_index("kern")
    rows = mask_hbm.shape[0]
    margin = (span - 1) // 2
    depth = -(-span * PITCH // 128) * 128
    has_up = tile > 0
    has_down = tile < tile_count - 1

    barrier = pltpu.get_barrier_semaphore()
    for step in range(1, kern_count):
        peer = lax.rem(kern + step, kern_count)
        pl.semaphore_signal(barrier, inc=1, device_id=(tile, peer), device_id_type=MESH)

    @pl.when(has_up)
    def _():
        pl.semaphore_signal(barrier, inc=1, device_id=(tile - 1, kern), device_id_type=MESH)

    @pl.when(has_down)
    def _():
        pl.semaphore_signal(barrier, inc=1, device_id=(tile + 1, kern), device_id_type=MESH)

    small_loads = [
        pltpu.make_async_copy(kernel_hbm, kernel_ref, load_sem.at[2]),
        pltpu.make_async_copy(assign_hbm, assign_own, load_sem.at[3]),
    ]
    loads, finish = window_of(
        mask_hbm, target_hbm, mask_window, target_window, load_sem, share, margin
    )
    for load in small_loads + loads:
        load.start()

    square[...] = jnp.zeros_like(square)
    for load in small_loads:
        load.wait()
    for row in range(span):
        pair = kernel_ref[row].astype(jnp.float32)
        square[0, row : row + 1, 0:span] = pair[0:1]
        square[1, row : row + 1, 0:span] = pair[1:2]
    lane = lax.broadcasted_iota(jnp.int32, (1, 128), 1)
    chunk_count = depth // 128
    for part in range(2):
        turned = square[part].T
        chunks = [jnp.zeros((1, 128), jnp.float32)] * chunk_count
        for column in range(span):
            chunk, offset = divmod(column * PITCH, 128)
            row = turned[column : column + 1]
            row = pltpu.roll(row, offset, 1) if offset else row
            if offset + span <= 128:
                chunks[chunk] = chunks[chunk] + row
            else:
                chunks[chunk] = chunks[chunk] + jnp.where(lane >= offset, row, 0.0)
                chunks[chunk + 1] = chunks[chunk + 1] + jnp.where(lane < offset, row, 0.0)
        mark = assign_own[0].astype(jnp.float32)
        chunks[-1] = jnp.where(lane >= 112, mark, chunks[-1])
        for chunk in range(chunk_count):
            tap_rows[8 * part + chunk : 8 * part + chunk + 1, :] = chunks[chunk]
    own_taps[...] = tap_rows[...].astype(jnp.bfloat16)

    own_copy = pltpu.make_async_copy(own_taps, all_taps.at[0], own_sem.at[0])
    own_copy.start()
    mask_own, target_own = finish()
    own_image[0:rows, :] = mask_own
    own_image[rows:, :] = target_own
    image_copy = pltpu.make_async_copy(own_image, own_rows, own_sem.at[1])
    image_copy.start()
    send_up[0:MASK_HALO, :] = mask_own[0:MASK_HALO]
    send_up[MASK_HALO:, :] = target_own[0:TARGET_HALO]
    send_down[0:MASK_HALO, :] = mask_own[rows - MASK_HALO :]
    send_down[MASK_HALO:, :] = target_own[rows - TARGET_HALO :]
    upward = pltpu.make_async_remote_copy(
        src_ref=send_up,
        dst_ref=below,
        send_sem=halo_send.at[0],
        recv_sem=halo_recv.at[0],
        device_id=(tile - 1, kern),
        device_id_type=MESH,
    )
    downward = pltpu.make_async_remote_copy(
        src_ref=send_down,
        dst_ref=above,
        send_sem=halo_send.at[1],
        recv_sem=halo_recv.at[1],
        device_id=(tile + 1, kern),
        device_id_type=MESH,
    )
    pl.semaphore_wait(barrier, kern_count - 1 + has_up.astype(jnp.int32) + has_down.astype(jnp.int32))
    tap_copies = []
    for step in range(1, kern_count):
        peer = lax.rem(kern + step, kern_count)
        tap_copies.append(
            pltpu.make_async_remote_copy(
                src_ref=own_taps,
                dst_ref=all_taps.at[step],
                send_sem=tap_send.at[step],
                recv_sem=tap_recv.at[step],
                device_id=(tile, peer),
                device_id_type=MESH,
            )
        )
    for copy in tap_copies:
        copy.start()
    pl.when(has_up)(upward.start)
    pl.when(has_down)(downward.start)
    own_copy.wait()
    image_copy.wait()
    for copy in tap_copies:
        copy.wait()
    pl.when(has_up)(upward.wait_send)
    pl.when(has_down)(downward.wait_send)
    pl.when(has_up)(downward.wait_recv)
    pl.when(has_down)(upward.wait_recv)


def gradient_kernel(
    sizes, own_hbm, weight_hbm, taps_hbm, above_hbm, below_hbm, grad_out, resist_out,
    own_image, weight_ref, all_taps, above, below, mask_rows, target_rows, toeplitz,
    shifted, fields, adjoint, spread, resist_rows, grad_rows, resist_own, grad_own, load_sem, store_sem,
):
    kern_count, tile_count, span, share, clip_cols = sizes
    tile = lax.axis_index("tile")
    kern = lax.axis_index("kern")
    rows = own_hbm.shape[0] // 2
    clip_rows = rows * tile_count
    margin = (span - 1) // 2
    height = (rows + 2 * margin) // BLOCKS
    padded = -(-height // 16) * 16
    depth = toeplitz.shape[1]
    chunk_count = depth // 128
    reach = share + 4 * margin
    width = above.shape[1]
    lanes = shifted.shape[1]

    own_load = pltpu.make_async_copy(own_hbm, own_image, load_sem.at[0])
    halo_loads = [
        pltpu.make_async_copy(above_hbm, above, load_sem.at[2]),
        pltpu.make_async_copy(below_hbm, below, load_sem.at[3]),
    ]
    tap_loads = [
        pltpu.make_async_copy(taps_hbm, all_taps, load_sem.at[4]),
        pltpu.make_async_copy(weight_hbm, weight_ref, load_sem.at[5]),
    ]
    for load in [own_load] + halo_loads + tap_loads:
        load.start()

    own_load.wait()
    mask_rows[MASK_HALO : MASK_HALO + rows, :] = own_image[0:rows, :].astype(jnp.float32)
    target_rows[TARGET_HALO : TARGET_HALO + rows, :] = own_image[rows:, :].astype(jnp.float32)
    for load in halo_loads:
        load.wait()
    for halo, inside, mask_at, target_at in (
        (above, tile > 0, 0, 0),
        (below, tile < tile_count - 1, MASK_HALO + rows, TARGET_HALO + rows),
    ):
        held = jnp.where(inside, halo[...].astype(jnp.float32), 0.0)
        mask_rows[mask_at : mask_at + MASK_HALO, :] = held[0:MASK_HALO]
        target_rows[target_at : target_at + TARGET_HALO, :] = held[MASK_HALO:]

    def side_by_side(held, top, count, shift):
        pieces = []
        for block in range(BLOCKS):
            piece = held[top + block * height : top + block * height + count, :]
            piece = pltpu.roll(piece, width - shift, 1) if shift else piece
            pieces.append(piece[:, :reach])
        if lanes > BLOCKS * reach:
            pieces.append(jnp.zeros((count, lanes - BLOCKS * reach), jnp.float32))
        return jnp.concatenate(pieces, axis=1)

    window = side_by_side(mask_rows, MASK_HALO - 2 * margin, PITCH, 0)
    for column in range(span):
        turned = window if column == 0 else pltpu.roll(window, lanes - column, 1)
        shifted[column * PITCH : (column + 1) * PITCH, :] = turned.astype(jnp.bfloat16)
    shifted[span * PITCH :, :] = jnp.zeros((depth - span * PITCH, lanes), jnp.bfloat16)

    for load in tap_loads:
        load.wait()
    weights = weight_ref[...]
    total = jnp.sum(weights, axis=1, keepdims=True)
    slot_ids = lax.broadcasted_iota(jnp.int32, weights.shape, 1).astype(jnp.float32)
    own_lane = lax.broadcasted_iota(jnp.int32, (padded, 128), 1)
    own_row = lax.broadcasted_iota(jnp.int32, (padded, 128), 0)
    same_chunk = own_lane >= own_row
    shares = []
    for source in range(kern_count):
        block = all_taps[source].astype(jnp.float32)
        picked = jnp.where(slot_ids == block[7:8, 112:113], weights, 0.0)
        shares.append(jnp.sum(picked, axis=1, keepdims=True) / total)
        for part in range(2):
            first = (2 * source + part) * padded
            before = jnp.zeros((padded, 128), jnp.float32)
            for chunk in range(chunk_count):
                at = 8 * part + chunk
                row = jnp.broadcast_to(block[at : at + 1], (padded, 128))
                turned = pltpu.roll(row, 0, 1, stride=1, stride_axis=0)
                toeplitz[first : first + padded, chunk * 128 : (chunk + 1) * 128] = jnp.where(
                    same_chunk, turned, before
                ).astype(jnp.bfloat16)
                before = turned

    fields[...] = jnp.dot(toeplitz[...], shifted[...], preferred_element_type=jnp.float32)

    row_at = lax.broadcasted_iota(jnp.int32, (padded, lanes), 0)
    col_at = lax.broadcasted_iota(jnp.int32, (padded, lanes), 1)
    clip_row = tile * rows - margin + row_at
    clip_col = kern * share - margin + col_at
    for block in range(1, BLOCKS):
        later = col_at >= block * reach
        clip_row = jnp.where(later, clip_row + height, clip_row)
        clip_col = jnp.where(later, clip_col - reach, clip_col)
    inside = jnp.logical_and(
        jnp.logical_and(clip_row >= 0, clip_row < clip_rows),
        jnp.logical_and(clip_col >= 0, clip_col < clip_cols),
    )
    inside = jnp.logical_and(inside, row_at < height)
    target = side_by_side(target_rows, TARGET_HALO - margin, padded, margin)
    aerial = jnp.zeros((padded, lanes), jnp.float32)
    for source in range(kern_count):
        first = 2 * source * padded
        real = fields[first : first + padded, :]
        imag = fields[first + padded : first + 2 * padded, :]
        aerial = aerial + shares[source] * (real * real + imag * imag)
    resist = 1.0 / (1.0 + jnp.exp(-SLOPE_FACTOR * (aerial - LEVEL_VALUE)))
    sense = 2.0 * (resist - target) * SLOPE_FACTOR * resist * (1.0 - resist)
    sense = jnp.where(inside, sense, 0.0)
    for source in range(kern_count):
        scaled = (2.0 * shares[source]) * sense
        for part in range(2):
            first = (2 * source + part) * padded
            adjoint[first : first + padded, :] = (
                scaled * fields[first : first + padded, :]
            ).astype(jnp.bfloat16)
    for block in range(BLOCKS):
        piece = pltpu.roll(resist, lanes - block * reach - margin, 1)[:, :share]
        resist_rows[block * height : block * height + padded, :] = piece
    resist_own[...] = resist_rows[margin : margin + rows, :]
    resist_store = pltpu.make_async_copy(resist_own, resist_out, store_sem.at[0])
    resist_store.start()

    spread[...] = lax.dot_general(
        toeplitz[...], adjoint[...], (((0,), (0,)), ((), ())), preferred_element_type=jnp.float32
    )

    gathered = spread[0:PITCH, :]
    for column in range(1, span):
        place = column * PITCH
        gathered = gathered + pltpu.roll(spread[place : place + PITCH, :], column, 1)
    grad_rows[...] = jnp.zeros_like(grad_rows)
    for block in range(BLOCKS):
        piece = pltpu.roll(gathered, lanes - block * reach - 2 * margin, 1)[:, :share]
        grad_rows[block * height : block * height + PITCH, :] += piece
    grad_own[...] = grad_rows[2 * margin : 2 * margin + rows, :]
    grad_store = pltpu.make_async_copy(grad_own, grad_out, store_sem.at[1])
    grad_store.start()

    resist_store.wait()
    grad_store.wait()


def on_device(mask, target, kernels, source_weight, assign):
    rows, col_count = mask.shape
    span = kernels.shape[-1]
    margin = (span - 1) // 2
    kern_count = lax.axis_size("kern")
    tile_count = lax.axis_size("tile")
    share = col_count // kern_count
    reach = share + 4 * margin
    width = -(-reach // 128) * 128
    lanes = -(-BLOCKS * reach // 128) * 128
    depth = -(-span * PITCH // 128) * 128
    height = (rows + 2 * margin) // BLOCKS
    padded = -(-height // 16) * 16
    parts = 2 * kern_count
    halo = MASK_HALO + TARGET_HALO
    sizes = (kern_count, tile_count, span, share)
    limit = 56 * 1024 * 1024
    by_row = jnp.swapaxes(kernels[0], 0, 1)
    taps, above, below, own_rows = pl.pallas_call(
        functools.partial(exchange_kernel, sizes),
        out_shape=(
            jax.ShapeDtypeStruct((kern_count, 16, 128), jnp.bfloat16),
            jax.ShapeDtypeStruct((halo, width), jnp.bfloat16),
            jax.ShapeDtypeStruct((halo, width), jnp.bfloat16),
            jax.ShapeDtypeStruct((2 * rows, width), jnp.bfloat16),
        ),
        in_specs=[IN_ANY] * 4,
        out_specs=(IN_ANY,) * 4,
        scratch_shapes=[
            pltpu.VMEM((rows, width + 128), jnp.float32),
            pltpu.VMEM((rows, width + 128), jnp.int32),
            pltpu.VMEM((halo, width), jnp.bfloat16),
            pltpu.VMEM((halo, width), jnp.bfloat16),
            pltpu.VMEM((2, 128, 128), jnp.float32),
            pltpu.VMEM((16, 128), jnp.float32),
            pltpu.VMEM((16, 128), jnp.bfloat16),
            pltpu.VMEM(by_row.shape, by_row.dtype),
            pltpu.SMEM((1,), jnp.int32),
            pltpu.VMEM((2 * rows, width), jnp.bfloat16),
            pltpu.SemaphoreType.DMA((4,)),
            pltpu.SemaphoreType.DMA((2,)),
            pltpu.SemaphoreType.DMA((kern_count,)),
            pltpu.SemaphoreType.DMA((kern_count,)),
            pltpu.SemaphoreType.DMA((2,)),
            pltpu.SemaphoreType.DMA((2,)),
        ],
        compiler_params=pltpu.CompilerParams(
            collective_id=0, has_side_effects=True, vmem_limit_bytes=limit
        ),
        name="exchange",
    )(mask, target, by_row, assign)
    image = jax.ShapeDtypeStruct((rows, share), jnp.float32)
    return pl.pallas_call(
        functools.partial(gradient_kernel, sizes + (col_count,)),
        out_shape=(image, image),
        in_specs=[IN_ANY] * 5,
        out_specs=(IN_ANY, IN_ANY),
        scratch_shapes=[
            pltpu.VMEM((2 * rows, width), jnp.bfloat16),
            pltpu.VMEM((1, source_weight.shape[0]), jnp.float32),
            pltpu.VMEM((kern_count, 16, 128), jnp.bfloat16),
            pltpu.VMEM((halo, width), jnp.bfloat16),
            pltpu.VMEM((halo, width), jnp.bfloat16),
            pltpu.VMEM((rows + 2 * MASK_HALO, width), jnp.float32),
            pltpu.VMEM((rows + 2 * TARGET_HALO, width), jnp.float32),
            pltpu.VMEM((parts * padded, depth), jnp.bfloat16),
            pltpu.VMEM((depth, lanes), jnp.bfloat16),
            pltpu.VMEM((parts * padded, lanes), jnp.float32),
            pltpu.VMEM((parts * padded, lanes), jnp.bfloat16),
            pltpu.VMEM((depth, lanes), jnp.float32),
            pltpu.VMEM(((BLOCKS - 1) * height + padded, share), jnp.float32),
            pltpu.VMEM(((BLOCKS - 1) * height + PITCH, share), jnp.float32),
            pltpu.VMEM((rows, share), jnp.float32),
            pltpu.VMEM((rows, share), jnp.float32),
            pltpu.SemaphoreType.DMA((6,)),
            pltpu.SemaphoreType.DMA((2,)),
        ],
        compiler_params=pltpu.CompilerParams(vmem_limit_bytes=limit),
        name="image_gradient",
    )(own_rows, source_weight[None, :], taps, above, below)


def solution(mesh):
    placed = (P("tile", None), P("tile", None), P("kern", None, None, None), P(), P("kern"))
    return jax.shard_map(
        on_device,
        mesh=mesh,
        in_specs=placed,
        out_specs=(P("tile", "kern"), P("tile", "kern")),
        check_vma=False,
    )
```
